128 devices in a mesh: row: 4 (over x), col: 32 (over y, z, core).
Axes of the slice: x: 4, y: 4, z: 4, core: 2. Of those that a mesh axis runs over, the one named last changes fastest.
Arguments:
- front: float32 [8, 4, 256, 1, 32, 256], P(None, 'row', None, None, 'col'), as said below
- child_tiles: float32 [4, 32, 32, 256, 256], P('row', 'col'), may hold values from -0.875 to 0.875
- child_owner: int32 [4, 32, 32], P('row', 'col'), may hold values from 0 to 31, each once within a row
- child_place: int32 [4, 32, 32], P('row', 'col'), may hold values from 0 to 7
- child_count: int32 [4, 32], P('row', 'col'), may hold values from 24 to 32, as said below
- tile_mask: int32 [32], replicated, may hold values from 0 to 1, as said below
Outputs:
- factored: float32 [8, 4, 256, 1, 32, 256], P(None, 'row', None, None, 'col')
The draws below stay inside these ranges and needn't reach their ends.
Inputs may be any that keep to these rules, and one draw needn't show every extreme that they name: `child_owner`: each device names every column device exactly once among its 32 slots. `child_count`: some device has all 32 slots live. `front`: symmetric positive definite; its leading 2 * 512 rows and columns stay positive definite after the children are added. `tile_mask`: among the tile rows below all panels, some entry is 0 and some is 1.
All inputs are finite; a program needn't handle non-finite values.
Results may differ from the reference program's by a relative error of at most 0.0001.
Values sent between devices are 32-bit elements; how exact they have to be, the bound alone decides.
A program may use at most 128 MiB of HBM per device.

```python
import math
import jax
import jax.numpy as jnp
from jax import lax

TILE = 256
PANEL = 512
NPANEL = 2
TC = 1
NT = 32
TR = 8
ORDER = 8192
CAP = 32
N_ROW = 4
N_COL = 32


def draw_front(key, part):
    order = NT * TILE
    inner = 4 * PANEL
    base = jax.random.normal(key, (order, inner), jnp.float32)
    whole = jnp.dot(base, base.T, precision=lax.Precision.HIGHEST) * (1.0 / math.sqrt(inner))
    shift = jax.random.uniform(jax.random.fold_in(key, 7), (order,), jnp.float32, 0.4, 0.8) * math.sqrt(inner)
    idx = jnp.arange(order)
    whole = whole.at[idx, idx].add(shift)
    return whole.reshape(TR, N_ROW, TILE, TC, N_COL, TILE)


def draw_child_count(key, part):
    counts = jax.random.randint(key, (N_ROW * N_COL,), 3 * CAP // 4, CAP + 1)
    chosen = jax.random.randint(jax.random.fold_in(key, 3), (), 0, N_ROW * N_COL)
    counts = jnp.where(jnp.arange(N_ROW * N_COL) == chosen, CAP, counts)
    return counts.reshape(N_ROW, N_COL).astype(jnp.int32)


def draw_tile_mask(key, part):
    bits = jax.random.randint(key, (NT,), 0, 2)
    start = NPANEL * PANEL // TILE
    span = NT - start
    first_pick = jax.random.randint(jax.random.fold_in(key, 5), (), 0, span)
    step_pick = jax.random.randint(jax.random.fold_in(key, 6), (), 0, span - 1)
    second_pick = (first_pick + 1 + step_pick) % span
    idx = jnp.arange(NT)
    bits = jnp.where(idx == first_pick + start, 0, bits)
    bits = jnp.where(idx == second_pick + start, 1, bits)
    return bits.astype(jnp.int32)


def plant(drawn, rng, low, top_value):
    extent = drawn.shape
    index_at = [jax.random.randint(jax.random.fold_in(rng, axis), (), 0, extent[axis]) for axis in range(len(extent))]
    drawn = drawn.at[tuple(index_at)].set(low)
    longest = extent.index(max(extent))
    index_at[longest] = (index_at[longest] + 1) % extent[longest]
    return drawn.at[tuple(index_at)].set(top_value)


def block_levels(stream_key, extent, split, least, high):
    def one(dim, parts):
        steps = jax.random.uniform(jax.random.fold_in(jax.random.fold_in(stream_key, 6), dim), (parts,), jnp.float32, least / len(split), high / len(split))
        return jnp.repeat(jnp.exp(steps), extent[dim] // parts).reshape((-1,) + (1,) * (len(extent) - dim - 1))

    factor_of = one(*split[0])
    for cut in split[1:]:
        factor_of = factor_of * one(*cut)
    return factor_of


def centred(stream_key, extent, width, limit, shards=(), kind=jnp.bfloat16):
    array = jax.random.normal(stream_key, extent, jnp.float32) * width
    if len(shards) > 0:
        array = block_levels(stream_key, extent, shards, -0.22, 0.18) * array
    return jnp.clip(array, min=-limit, max=limit).astype(kind)


def setup_inputs(seed: int = 0) -> dict:
    key_list = jax.random.split(jax.random.key(seed), 7)
    return {
        "front": draw_front(jax.random.fold_in(key_list[6], 71), 0),
        "child_tiles": centred(key_list[1], (N_ROW, N_COL, CAP, TILE, TILE), (0.12 * TC * N_ROW ** -0.5), 0.875, ((0, 4), (1, 32)), jnp.float32),
        "child_owner": jax.vmap(lambda own: jax.random.permutation(own, N_COL))(jax.random.split(key_list[2], N_ROW * N_COL)).reshape((N_ROW, N_COL, CAP)).astype(jnp.int32),
        "child_place": plant(jax.random.randint(key_list[3], (N_ROW, N_COL, CAP), 0, TR * TC), jax.random.fold_in(key_list[3], 1), 0, (TR * TC) - 1).astype(jnp.int32),
        "child_count": draw_child_count(jax.random.fold_in(key_list[6], 71), 0),
        "tile_mask": draw_tile_mask(jax.random.fold_in(key_list[6], 71), 0),
    }


def reference(front, child_tiles, child_owner, child_place, child_count, tile_mask):
    tiles = front.transpose(0, 1, 3, 4, 2, 5)
    owner = child_owner
    slot_ids = jnp.arange(CAP, dtype=jnp.int32)
    valid = (slot_ids[None, None, :] < child_count[:, :, None]).astype(jnp.float32)
    row_ids = jnp.broadcast_to(jnp.arange(N_ROW, dtype=jnp.int32)[:, None, None], owner.shape)
    tile_row = child_place // TC
    tile_col = child_place % TC
    contrib = child_tiles * valid[..., None, None]
    tiles = tiles.at[tile_row, row_ids, tile_col, owner].add(contrib)
    whole = tiles.transpose(0, 1, 4, 2, 3, 5).reshape(ORDER, ORDER)
    panel_tiles = NPANEL * PANEL // TILE
    keep_tiles = (tile_mask == 1) | (jnp.arange(NT, dtype=jnp.int32) < panel_tiles)
    row_mask = jnp.repeat(keep_tiles.astype(jnp.float32), TILE)
    ident = jnp.eye(PANEL, dtype=jnp.float32)
    for step in range(NPANEL):
        low = step * PANEL
        high = low + PANEL
        factor = jnp.linalg.cholesky(whole[low:high, low:high])
        inverse = jax.scipy.linalg.solve_triangular(factor, ident, lower=True)
        masked = whole[high:, low:high] * row_mask[high:, None]
        lower = jnp.dot(masked, inverse.T, precision=lax.Precision.HIGHEST)
        update = jnp.dot(lower, lower.T, precision=lax.Precision.HIGHEST)
        whole = whole.at[high:, high:].add(-update)
        whole = whole.at[low:high, low:high].set(factor)
        whole = whole.at[high:, low:high].set(lower)
        whole = whole.at[low:high, high:].set(0.0)
    return whole.reshape(TR, N_ROW, TILE, TC, N_COL, TILE)
```

```python
import jax
import jax.numpy as jnp
from jax import lax
from jax.experimental import pallas as pl
from jax.experimental.pallas import tpu as pltpu
from jax.sharding import PartitionSpec as P

HI = lax.Precision.HIGHEST
NB = 128
SB = 32
TILE = 256
MIB = 1024 * 1024

def dot_nt(a, b):
    return lax.dot_general(a, b, (((1,), (1,)), ((), ())), precision=HI, preferred_element_type=jnp.float32)

def dot_tn(a, b):
    return lax.dot_general(a, b, (((0,), (0,)), ((), ())), precision=HI, preferred_element_type=jnp.float32)

def invert_factor(block):
    sub = lax.broadcasted_iota(jnp.int32, (NB, NB), 0)
    lane = lax.broadcasted_iota(jnp.int32, (NB, NB), 1)
    eye = (sub == lane).astype(jnp.float32)
    rest = jnp.concatenate([block, eye], axis=1)
    done = []
    for sb in range(NB // SB):
        w = rest[:SB]
        rows = []
        for t in range(SB // 8):
            base = sb * SB + t * 8
            h = w.shape[0]
            ids = lax.broadcasted_iota(jnp.int32, (h, NB), 0)
            cols = [jnp.broadcast_to(w[:, base + i:base + i + 1], (h, NB)) for i in range(8)]
            final = []
            for j in range(8):
                cj = cols[j]
                piv = jnp.broadcast_to(cj[j:j + 1], (8, NB))
                rs = lax.rsqrt(piv)
                rs_h = jnp.concatenate([rs] * (h // 8), axis=0)
                inv = rs * rs
                inv_h = jnp.concatenate([inv] * (h // 8), axis=0)
                for i in range(j + 1, 8):
                    ci = jnp.broadcast_to(cj[i:i + 1], (h, NB))
                    cols[i] = cols[i] - cj * (ci * inv_h)
                lj = jnp.where(ids > j, cj * rs_h, 0.0)
                r = w[j:j + 1] * jnp.concatenate([rs[:1], rs[:1]], axis=1)
                final.append(r)
                lw = jnp.concatenate([lj, lj], axis=1)
                w = w - lw * jnp.broadcast_to(r, (h, 2 * NB))
            rows.append(jnp.concatenate(final, axis=0))
            w = w[8:]
        r = jnp.concatenate(rows, axis=0)
        done.append(r[:, NB:])
        if sb + 1 < NB // SB:
            lo = (sb + 1) * SB
            rest = rest[SB:] - dot_tn(r[:, lo:NB], r)
    return jnp.concatenate(done, axis=0)

def chol_body(where_ref, diag_ref, own_ref, out_ref, s):
    n = diag_ref.shape[0]
    m = own_ref.shape[0]
    nb = n // NB
    half = nb // 2
    for a in range(nb):
        for b in range(a + 1):
            x = diag_ref[a * NB:(a + 1) * NB, b * NB:(b + 1) * NB]
            if a // half == b // half:
                y = diag_ref[b * NB:(b + 1) * NB, a * NB:(a + 1) * NB]
                x = (x + y.T) * 0.5
            s[a * NB:(a + 1) * NB, b * NB:(b + 1) * NB] = x
        if a + 1 < nb:
            s[a * NB:(a + 1) * NB, (a + 1) * NB:] = jnp.zeros((NB, n - (a + 1) * NB), jnp.float32)
    row0 = where_ref[0]
    s[n:n + 8, :] = s[pl.ds(pl.multiple_of(row0, 8), 8), :]
    for t in range(1, m // 8):
        s[n + 8 * t:n + 8 * t + 8, :] = jnp.where(where_ref[t] > 0, own_ref[8 * t:8 * t + 8, :], 0.0)
    for k in range(nb):
        lo = k * NB
        hi = lo + NB
        inv = invert_factor(s[lo:hi, lo:hi])
        x = dot_nt(s[hi:, lo:hi], inv)
        s[hi:, lo:hi] = x
        at = hi
        while at < n:
            width = NB if at == hi else min(2 * NB, n - at)
            s[at:, at:at + width] = s[at:, at:at + width] - dot_nt(x[at - hi:], x[at - hi:at - hi + width])
            at += width
    res = s[n:, :]
    ids = lax.broadcasted_iota(jnp.int32, (m, n), 0)
    lane = lax.broadcasted_iota(jnp.int32, (m, n), 1)
    out_ref[...] = jnp.where((ids >= 8) | (lane <= ids + row0), res, 0.0)

def chol_call(where, diag, own):
    n, m = diag.shape[0], own.shape[0]
    return pl.pallas_call(
        chol_body,
        out_shape=jax.ShapeDtypeStruct((m, n), jnp.float32),
        in_specs=[pl.BlockSpec(memory_space=pltpu.SMEM), pl.BlockSpec(memory_space=pltpu.VMEM), pl.BlockSpec(memory_space=pltpu.VMEM)],
        out_specs=pl.BlockSpec(memory_space=pltpu.VMEM),
        scratch_shapes=[pltpu.VMEM((n + m, n), jnp.float32)],
        compiler_params=pltpu.CompilerParams(vmem_limit_bytes=32 * 1024 * 1024),
        cost_estimate=pl.CostEstimate(flops=60_000_000_000, bytes_accessed=5_000_000, transcendentals=0),
    )(where, diag, own)


def pack_body(slot_ref, tile_ref, out_ref):
    out_ref[...] = tile_ref[...]


def pack_call(slots, tiles):
    n = slots.shape[0]
    t = tiles.shape[1]
    return pl.pallas_call(
        pack_body,
        out_shape=jax.ShapeDtypeStruct((n, t, t), tiles.dtype),
        grid_spec=pltpu.PrefetchScalarGridSpec(
            num_scalar_prefetch=1,
            grid=(n,),
            in_specs=[pl.BlockSpec((1, t, t), lambda q, slot: (slot[q], 0, 0))],
            out_specs=pl.BlockSpec((1, t, t), lambda q, slot: (q, 0, 0)),
        ),
        cost_estimate=pl.CostEstimate(flops=0, bytes_accessed=n * t * t * 8, transcendentals=0),
    )(slots, tiles)


def panel_body(got_ref, front_ref, out_ref):
    sources, slab, _ = got_ref.shape
    lead = front_ref.shape[1]
    for q in range(4):
        at = slice(q * TILE, (q + 1) * TILE)
        acc = [front_ref[q, t] for t in range(lead)]
        for s in range(sources):
            label = got_ref[s, q:q + 1, 5 * TILE:5 * TILE + 128]
            label = jnp.broadcast_to(jnp.concatenate([label, label], axis=1), (slab, TILE))
            part = got_ref[s, :, at]
            for t in range(lead):
                acc[t] = acc[t] + jnp.where(label == float(t), part, 0.0)
        for t in range(lead):
            out_ref[t * slab:(t + 1) * slab, at] = acc[t]


def panel_call(got, front_part):
    lead, slab = front_part.shape[1], front_part.shape[2]
    return pl.pallas_call(
        panel_body,
        out_shape=jax.ShapeDtypeStruct((lead * slab, 4 * TILE), jnp.float32),
        cost_estimate=pl.CostEstimate(flops=0, bytes_accessed=got.size * 4, transcendentals=0),
    )(got, front_part)


def add_body(label_ref, front_ref, got_ref, out_ref):
    out_ref[...] = front_ref[...]

    def step(s, carry):
        p = label_ref[s]

        @pl.when(p >= 0)
        def _():
            out_ref[p] = out_ref[p] + got_ref[s]

        return carry

    lax.fori_loop(0, got_ref.shape[0], step, 0)


def add_call(labels, front, got):
    lead = front.shape[0]
    n = got.shape[0]
    rows = 32
    return pl.pallas_call(
        add_body,
        out_shape=jax.ShapeDtypeStruct(front.shape, jnp.float32),
        grid_spec=pltpu.PrefetchScalarGridSpec(
            num_scalar_prefetch=1,
            grid=(TILE // rows,),
            in_specs=[
                pl.BlockSpec((lead, rows, TILE), lambda i, _: (0, i, 0)),
                pl.BlockSpec((n, rows, TILE), lambda i, _: (0, i, 0)),
            ],
            out_specs=pl.BlockSpec((lead, rows, TILE), lambda i, _: (0, i, 0)),
        ),
        cost_estimate=pl.CostEstimate(flops=0, bytes_accessed=(n + 2 * lead) * TILE * TILE * 4, transcendentals=0),
    )(labels, front, got)


def split(x):
    high = x.astype(jnp.bfloat16)
    low = (x - high.astype(jnp.float32)).astype(jnp.bfloat16)
    return high, low


def nt(a, b):
    return lax.dot_general(a, b, (((1,), (1,)), ((), ())), preferred_element_type=jnp.float32)


def final_body(col_ref, acc_ref, l_ref, across_ref, out_ref):
    c = col_ref[0]
    t = pl.program_id(0)
    n = across_ref.shape[1]

    @pl.when(c < 4)
    def _():
        at = pl.multiple_of(jnp.minimum(c, 3) * TILE, TILE)
        out_ref[0] = l_ref[:, 0, :, pl.ds(at, TILE)].reshape(TILE, TILE)

    @pl.when((c >= 4) & (t == 0))
    def _():
        out_ref[...] = jnp.zeros_like(out_ref)

    @pl.when((c >= 4) & (t > 0))
    def _():
        ah, al = split(l_ref[...].reshape(TILE, n))
        bh, bl = split(across_ref[...])
        out_ref[0] = acc_ref[0] - (nt(ah, bh) + (nt(ah, bl) + nt(al, bh)))


def final_call(col, acc, gathered, across):
    lead = acc.shape[0]
    j, _, slab, n = gathered.shape
    return pl.pallas_call(
        final_body,
        out_shape=jax.ShapeDtypeStruct(acc.shape, jnp.float32),
        grid_spec=pltpu.PrefetchScalarGridSpec(
            num_scalar_prefetch=1,
            grid=(lead,),
            in_specs=[
                pl.BlockSpec((1, TILE, TILE), lambda i, _: (i, 0, 0)),
                pl.BlockSpec((j, 1, slab, n), lambda i, _: (0, i, 0, 0)),
                pl.BlockSpec((TILE, n), lambda i, _: (0, 0)),
            ],
            out_specs=pl.BlockSpec((1, TILE, TILE), lambda i, _: (i, 0, 0)),
        ),
        compiler_params=pltpu.CompilerParams(vmem_limit_bytes=32 * MIB),
        cost_estimate=pl.CostEstimate(flops=6 * lead * TILE * TILE * n, bytes_accessed=gathered.size * 4, transcendentals=0),
    )(col, acc, gathered, across)


def local(front, child_tiles, child_owner, child_place, child_count, tile_mask):
    n_row = lax.axis_size("row")
    n_col = lax.axis_size("col")
    row_id = lax.axis_index("row")
    col_id = lax.axis_index("col")
    lead = front.shape[0]
    slab = TILE // n_col
    slots = child_tiles.shape[2]
    blocks = front.reshape(lead, TILE, TILE)
    tiles = child_tiles.reshape(slots, TILE, TILE)
    owner = child_owner.reshape(slots)
    place = child_place.reshape(slots)
    count = child_count.reshape(())
    ids = jnp.arange(slots, dtype=jnp.int32)
    hit = owner[None, :] == jnp.arange(n_col, dtype=jnp.int32)[:, None]
    slot_of = jnp.sum(jnp.where(hit, ids[None, :], 0), axis=1)
    label = jnp.sum(jnp.where(hit & (ids < count)[None, :], place[None, :] + 1, 0), axis=1) - 1
    label_f = label.astype(jnp.float32)

    panel_tiles = pack_call(slot_of[:4], tiles)
    slabs = panel_tiles.reshape(4, n_col, slab, TILE).transpose(1, 2, 0, 3).reshape(n_col, slab, 4 * TILE)
    mirrored = blocks[0].T.reshape(n_col, slab, TILE)
    marks = jnp.concatenate(
        [jnp.broadcast_to(label_f[None, :4], (n_col, 4)), label_f[:, None], jnp.zeros((n_col, slab - 5), jnp.float32)], axis=1
    )
    marks = jnp.broadcast_to(marks[:, :, None], (n_col, slab, 128))
    message = jnp.concatenate([slabs, mirrored, marks], axis=2)
    got = lax.all_to_all(message, "col", split_axis=0, concat_axis=0, tiled=True)
    cross = got[:, :, 4 * TILE:5 * TILE].reshape(lead, n_row, slab, TILE).transpose(1, 0, 2, 3)
    cross = lax.all_to_all(cross, "row", split_axis=0, concat_axis=0, tiled=True)
    own = panel_call(got, cross)

    payload = pack_call(slot_of, tiles)
    payload, got = lax.optimization_barrier((payload, got))
    arrived = lax.all_to_all(payload, "col", split_axis=0, concat_axis=0, tiled=True)

    diag = lax.all_gather(own[:slab], ("row", "col"), axis=0, tiled=True)
    row_tiles = jnp.arange(lead, dtype=jnp.int32) * n_row + row_id
    keep = jnp.sum(jnp.where(row_tiles[:, None] == jnp.arange(tile_mask.shape[0])[None, :], tile_mask[None, :], 0), axis=1)
    where = jnp.concatenate([(row_id * TILE + col_id * slab)[None], keep[1:]]).astype(jnp.int32)
    mine = chol_call(where, diag, own)
    gathered = lax.all_gather(mine, "col", axis=0, tiled=False).reshape(n_col, lead, slab, 4 * TILE)
    chosen = lax.dynamic_slice_in_dim(gathered, col_id // n_row, 1, axis=1).reshape(TILE, 4 * TILE)
    across = lax.psum(jnp.where(row_id == col_id % n_row, chosen, 0.0), "row")

    got_labels = got[:, 4, 5 * TILE].astype(jnp.int32)
    acc = add_call(got_labels, blocks, arrived)
    result = final_call(col_id.reshape(1), acc, gathered, across)
    return result.reshape(front.shape)


def solution(mesh):
    return jax.shard_map(
        local,
        mesh=mesh,
        in_specs=(
            P(None, "row", None, None, "col", None),
            P("row", "col", None, None, None),
            P("row", "col", None),
            P("row", "col", None),
            P("row", "col"),
            P(),
        ),
        out_specs=P(None, "row", None, None, "col", None),
        check_vma=False,
    )
```

```python
import jax
import jax.numpy as jnp
from jax import lax
from jax.experimental import pallas as pl
from jax.experimental.pallas import tpu as pltpu
from jax.sharding import PartitionSpec as P

HI = lax.Precision.HIGHEST
NB = 128
SB = 32
TILE = 256
MIB = 1024 * 1024
LATE = True

def dot_nt(a, b):
    return lax.dot_general(a, b, (((1,), (1,)), ((), ())), precision=HI, preferred_element_type=jnp.float32)

def dot_tn(a, b):
    return lax.dot_general(a, b, (((0,), (0,)), ((), ())), precision=HI, preferred_element_type=jnp.float32)

def invert_factor(block):
    sub = lax.broadcasted_iota(jnp.int32, (NB, NB), 0)
    lane = lax.broadcasted_iota(jnp.int32, (NB, NB), 1)
    eye = (sub == lane).astype(jnp.float32)
    rest = jnp.concatenate([block, eye], axis=1)
    done = []
    for sb in range(NB // SB):
        w = rest[:SB]
        rows = []
        for t in range(SB // 8):
            base = sb * SB + t * 8
            h = w.shape[0]
            ids = lax.broadcasted_iota(jnp.int32, (h, NB), 0)
            cols = [jnp.broadcast_to(w[:, base + i:base + i + 1], (h, NB)) for i in range(8)]
            final = []
            for j in range(8):
                cj = cols[j]
                piv = jnp.broadcast_to(cj[j:j + 1], (8, NB))
                rs = lax.rsqrt(piv)
                rs_h = jnp.concatenate([rs] * (h // 8), axis=0)
                inv = rs * rs
                inv_h = jnp.concatenate([inv] * (h // 8), axis=0)
                for i in range(j + 1, 8):
                    ci = jnp.broadcast_to(cj[i:i + 1], (h, NB))
                    cols[i] = cols[i] - cj * (ci * inv_h)
                lj = jnp.where(ids > j, cj * rs_h, 0.0)
                r = w[j:j + 1] * jnp.concatenate([rs[:1], rs[:1]], axis=1)
                final.append(r)
                lw = jnp.concatenate([lj, lj], axis=1)
                w = w - lw * jnp.broadcast_to(r, (h, 2 * NB))
            rows.append(jnp.concatenate(final, axis=0))
            w = w[8:]
        r = jnp.concatenate(rows, axis=0)
        done.append(r[:, NB:])
        if sb + 1 < NB // SB:
            lo = (sb + 1) * SB
            rest = rest[SB:] - dot_tn(r[:, lo:NB], r)
    return jnp.concatenate(done, axis=0)

def chol_body(where_ref, part_ref, own_ref, out_ref, s, diag_ref):
    n = diag_ref.shape[0]
    for q in range(4):
        rows = slice(q * TILE, (q + 1) * TILE)
        diag_ref[rows, :2 * TILE] = part_ref[:, :, :, q].reshape(TILE, 2 * TILE)
        if q >= 2:
            diag_ref[rows, 2 * TILE:] = part_ref[:, :, :, 2 + q].reshape(TILE, 2 * TILE)
    m = own_ref.shape[0]
    nb = n // NB
    half = nb // 2
    for a in range(nb):
        for b in range(a + 1):
            x = diag_ref[a * NB:(a + 1) * NB, b * NB:(b + 1) * NB]
            if a // half == b // half:
                y = diag_ref[b * NB:(b + 1) * NB, a * NB:(a + 1) * NB]
                x = (x + y.T) * 0.5
            s[a * NB:(a + 1) * NB, b * NB:(b + 1) * NB] = x
        if a + 1 < nb:
            s[a * NB:(a + 1) * NB, (a + 1) * NB:] = jnp.zeros((NB, n - (a + 1) * NB), jnp.float32)
    row0 = where_ref[0]
    s[n:n + 8, :] = s[pl.ds(pl.multiple_of(row0, 8), 8), :]
    for t in range(1, m // 8):
        s[n + 8 * t:n + 8 * t + 8, :] = jnp.where(where_ref[t] > 0, own_ref[8 * t:8 * t + 8, :], 0.0)
    for k in range(nb):
        lo = k * NB
        hi = lo + NB
        inv = invert_factor(s[lo:hi, lo:hi])
        x = dot_nt(s[hi:, lo:hi], inv)
        s[hi:, lo:hi] = x
        at = hi
        while at < n:
            width = NB if at == hi else min(2 * NB, n - at)
            s[at:, at:at + width] = s[at:, at:at + width] - dot_nt(x[at - hi:], x[at - hi:at - hi + width])
            at += width
    res = s[n:, :]
    ids = lax.broadcasted_iota(jnp.int32, (m, n), 0)
    lane = lax.broadcasted_iota(jnp.int32, (m, n), 1)
    out_ref[...] = jnp.where((ids >= 8) | (lane <= ids + row0), res, 0.0)

def chol_call(where, parts, own):
    m, n = own.shape
    vmem = pl.BlockSpec(memory_space=pltpu.VMEM)
    return pl.pallas_call(
        chol_body,
        out_shape=jax.ShapeDtypeStruct((m, n), jnp.float32),
        in_specs=[pl.BlockSpec(memory_space=pltpu.SMEM), vmem, vmem],
        out_specs=vmem,
        scratch_shapes=[pltpu.VMEM((n + m, n), jnp.float32), pltpu.VMEM((n, n), jnp.float32)],
        compiler_params=pltpu.CompilerParams(vmem_limit_bytes=56 * MIB),
        cost_estimate=pl.CostEstimate(flops=0, bytes_accessed=1000, transcendentals=0),
    )(where, parts, own)


MESH = pl.DeviceIdType.MESH


def here():
    r = lax.axis_index("row")
    c = lax.axis_index("col")
    return r, c, lax.div(c, 8), lax.rem(lax.div(c, 2), 4), lax.rem(c, 2)


def at_col(y, z, k):
    return (y * 4 + z) * 2 + k


def turn(i, d):
    return lax.rem(i + d, 4)


def greet(devices):
    barrier = pltpu.get_barrier_semaphore()
    for device in devices:
        pl.semaphore_signal(barrier, inc=1, device_id=device, device_id_type=MESH)
    pl.semaphore_wait(barrier, len(devices))


def plane_peers(r, y, z, k):
    out = [(r, at_col(y, z, 1 - k))]
    for d in range(1, 4):
        out.append((r, at_col(y, turn(z, d), k)))
        out.append((r, at_col(turn(y, d), z, k)))
    return out


def row_peers(r, c):
    return [(turn(r, d), c) for d in range(1, 4)]


def plane_gather(piece, send, recv, core_send, core_recv, r, y, z, k):
    def place(h, a, b):
        return (b, a) if h == 0 else (a, b)

    def axes(h):
        return (z, y) if h == 0 else (y, z)

    def push(h, da, db, to, send_sem, recv_sem):
        a, b = axes(h)
        ref = piece(h, *place(h, turn(a, 4 - da), turn(b, 4 - db)), k)
        copy = pltpu.make_async_remote_copy(
            src_ref=ref, dst_ref=ref, send_sem=send_sem, recv_sem=recv_sem, device_id=to, device_id_type=MESH
        )
        copy.start()
        return copy

    def along_first(h, d):
        a, b = axes(h)
        yy, zz = place(h, turn(a, d), b)
        return push(h, 0, 0, (r, at_col(yy, zz, k)), send.at[h, d, 0], recv.at[h, d, 0])

    def along_second(h, da, d):
        a, b = axes(h)
        yy, zz = place(h, a, turn(b, d))
        return push(h, da, 0, (r, at_col(yy, zz, k)), send.at[h, da, d], recv.at[h, da, d])

    def across(h, da, db):
        return push(h, da, db, (r, at_col(y, z, 1 - k)), core_send.at[h, da, db], core_recv.at[h, da, db])

    first, second, core = {}, {}, {}
    for d in range(1, 4):
        for h in range(2):
            first[h, d] = along_first(h, d)
    for d in range(1, 4):
        for h in range(2):
            second[h, 0, d] = along_second(h, 0, d)
    for h in range(2):
        core[h, 0, 0] = across(h, 0, 0)
    for da in range(1, 4):
        for h in range(2):
            first[h, da].wait_recv()
            for d in range(1, 4):
                second[h, da, d] = along_second(h, da, d)
            core[h, da, 0] = across(h, da, 0)
    for da in range(4):
        for db in range(1, 4):
            for h in range(2):
                second[h, da, db].wait_recv()
                core[h, da, db] = across(h, da, db)

    def finish():
        for copy in core.values():
            copy.wait_recv()
        for group in (first, second, core):
            for copy in group.values():
                copy.wait_send()

    return finish


def gather_sems():
    return [pltpu.SemaphoreType.DMA((2, 4, 4)) for _ in range(4)]


def rows_body(mine_ref, g_ref, across_ref, send, recv, core_send, core_recv, local_sem, x_send, x_recv):
    r, c, y, z, k = here()
    greet(plane_peers(r, y, z, k) + row_peers(r, c))
    keep = pltpu.make_async_copy(mine_ref, g_ref.at[y, z, k], local_sem.at[0])
    keep.start()
    keep.wait()
    half = mine_ref.shape[0] // 2

    def piece(h, yy, zz, kk):
        return g_ref.at[yy, zz, kk, pl.ds(h * half, half)]

    finish = plane_gather(piece, send, recv, core_send, core_recv, r, y, z, k)
    t = lax.div(c, 4)
    source = lax.rem(c, 4)

    def slab(kk):
        return g_ref.at[:, :, kk, t]

    def cross(i, kk, d):
        return pltpu.make_async_remote_copy(
            src_ref=slab(kk),
            dst_ref=across_ref.at[:, :, kk],
            send_sem=x_send.at[i, d],
            recv_sem=x_recv.at[i],
            device_id=(turn(r, d), c),
            device_id_type=MESH,
        )

    @pl.when(r == source)
    def _():
        for d in range(1, 4):
            cross(0, k, d).start()

    finish()

    @pl.when(r == source)
    def _():
        for d in range(1, 4):
            cross(1, 1 - k, d).start()
        own = pltpu.make_async_copy(g_ref.at[:, :, :, t], across_ref, local_sem.at[1])
        own.start()
        own.wait()
        for d in range(1, 4):
            cross(0, k, d).wait_send()
            cross(1, 1 - k, d).wait_send()

    @pl.when(r != source)
    def _():
        cross(0, k, 1).wait_recv()
        cross(1, 1 - k, 1).wait_recv()


def rows_call(mine):
    lead, slab, n = mine.shape
    return pl.pallas_call(
        rows_body,
        out_shape=[
            jax.ShapeDtypeStruct((4, 4, 2, lead, slab, n), jnp.float32),
            jax.ShapeDtypeStruct((4, 4, 2, slab, n), jnp.float32),
        ],
        in_specs=[pl.BlockSpec(memory_space=pl.ANY)],
        out_specs=[pl.BlockSpec(memory_space=pl.ANY)] * 2,
        scratch_shapes=gather_sems()
        + [pltpu.SemaphoreType.DMA((2,)), pltpu.SemaphoreType.DMA((2, 4)), pltpu.SemaphoreType.DMA((2,))],
        compiler_params=pltpu.CompilerParams(collective_id=1, has_side_effects=True, vmem_limit_bytes=56 * MIB),
        cost_estimate=pl.CostEstimate(flops=0, bytes_accessed=1000, transcendentals=0),
    )(mine)


def panel_body(message_ref, own_ref, diag_ref, got_ref, share, front, units, packed, msg_send, msg_recv, local_sem,
               f_send, f_recv, u_send, u_recv, send, recv, core_send, core_recv):
    r, c, y, z, k = here()
    n_col = got_ref.shape[0]
    slab = got_ref.shape[1]
    lead = share.shape[1]
    half = units.shape[3]
    greet([(r, lax.rem(c + d, n_col)) for d in range(1, n_col)] + row_peers(r, c))

    def message(d):
        to = lax.rem(c + d, n_col)
        return pltpu.make_async_remote_copy(
            src_ref=message_ref.at[to],
            dst_ref=got_ref.at[c],
            send_sem=msg_send.at[d],
            recv_sem=msg_recv.at[d],
            device_id=(r, to),
            device_id_type=MESH,
        )

    keep = pltpu.make_async_copy(message_ref.at[c], got_ref.at[c], local_sem.at[0])
    keep.start()
    for d in range(1, n_col):
        message(d).start()
    keep.wait()
    for d in range(1, n_col):
        message(d).wait_recv()

    def exchange(src, dst, s_sem, r_sem, d):
        return pltpu.make_async_remote_copy(
            src_ref=src, dst_ref=dst, send_sem=s_sem.at[d], recv_sem=r_sem.at[d], device_id=(turn(r, d), c),
            device_id_type=MESH,
        )

    for q in range(4):
        for t in range(lead):
            share[q, t] = got_ref[4 * t + q, :, 4 * TILE:5 * TILE]
    front[r] = share[r]
    shares = [exchange(share.at[turn(r, d)], front.at[r], f_send, f_recv, d) for d in range(1, 4)]
    for copy in shares:
        copy.start()
    own_ref[...] = jnp.zeros_like(own_ref)

    def add(s, carry):
        for q in range(4):
            at = slice(q * TILE, (q + 1) * TILE)
            label = got_ref[s, q:q + 1, 5 * TILE:5 * TILE + 128]
            label = jnp.broadcast_to(jnp.concatenate([label, label], axis=1), (slab, TILE))
            part = got_ref[s, :, at]
            for t in range(lead):
                rows = slice(t * slab, (t + 1) * slab)
                own_ref[rows, at] = own_ref[rows, at] + jnp.where(label == float(t), part, 0.0)
        return carry

    lax.fori_loop(0, n_col, add, 0)
    for copy in shares:
        copy.wait_recv()
    for q in range(4):
        at = slice(q * TILE, (q + 1) * TILE)
        for t in range(lead):
            rows = slice(t * slab, (t + 1) * slab)
            own_ref[rows, at] = own_ref[rows, at] + front[q, t]
    for p in range(2):
        units[r, p] = own_ref[:slab, p * half:(p + 1) * half]
    lines = [exchange(units.at[r], units.at[r], u_send, u_recv, d) for d in range(1, 4)]
    for copy in lines:
        copy.start()
    for copy in lines:
        copy.wait_recv()
    for q in range(4):
        packed[q] = units[q, 0]
    for q in range(2):
        packed[4 + q] = units[2 + q, 1]
    diag_ref[y, z, k] = packed[...]

    def piece(h, yy, zz, kk):
        return diag_ref.at[yy, zz, kk, pl.ds(h * 3, 3)]

    finish = plane_gather(piece, send, recv, core_send, core_recv, r, y, z, k)
    for d in range(1, n_col):
        message(d).wait_send()
    for copy in shares + lines:
        copy.wait_send()
    finish()


def panel_call(message, lead):
    n_col, slab, width = message.shape
    half = 2 * TILE
    dma = pltpu.SemaphoreType.DMA
    vmem = pl.BlockSpec(memory_space=pltpu.VMEM)
    return pl.pallas_call(
        panel_body,
        out_shape=[
            jax.ShapeDtypeStruct((lead * slab, 4 * TILE), jnp.float32),
            jax.ShapeDtypeStruct((4, 4, 2, 6, slab, half), jnp.float32),
            jax.ShapeDtypeStruct((n_col, slab, width), jnp.float32),
        ],
        in_specs=[vmem],
        out_specs=[vmem] * 3,
        scratch_shapes=[
            pltpu.VMEM((4, lead, slab, TILE), jnp.float32),
            pltpu.VMEM((4, lead, slab, TILE), jnp.float32),
            pltpu.VMEM((4, 2, slab, half), jnp.float32),
            pltpu.VMEM((6, slab, half), jnp.float32),
            dma((n_col,)),
            dma((n_col,)),
            dma((1,)),
            dma((4,)),
            dma((4,)),
            dma((4,)),
            dma((4,)),
        ]
        + gather_sems(),
        compiler_params=pltpu.CompilerParams(collective_id=0, has_side_effects=True, vmem_limit_bytes=56 * MIB),
        cost_estimate=pl.CostEstimate(flops=0, bytes_accessed=1000, transcendentals=0),
    )(message)


def pack_body(slot_ref, tile_ref, out_ref):
    out_ref[...] = tile_ref[...]


def pack_call(slots, tiles):
    n = slots.shape[0]
    t = tiles.shape[1]
    return pl.pallas_call(
        pack_body,
        out_shape=jax.ShapeDtypeStruct((n, t, t), tiles.dtype),
        grid_spec=pltpu.PrefetchScalarGridSpec(
            num_scalar_prefetch=1,
            grid=(n,),
            in_specs=[pl.BlockSpec((1, t, t), lambda q, slot: (slot[q], 0, 0))],
            out_specs=pl.BlockSpec((1, t, t), lambda q, slot: (q, 0, 0)),
        ),
        cost_estimate=pl.CostEstimate(flops=0, bytes_accessed=n * t * t * 8, transcendentals=0),
    )(slots, tiles)


def add_body(label_ref, front_ref, got_ref, out_ref):
    out_ref[...] = front_ref[...]

    def step(s, carry):
        p = label_ref[s]

        @pl.when(p >= 0)
        def _():
            out_ref[p] = out_ref[p] + got_ref[s]

        return carry

    lax.fori_loop(0, got_ref.shape[0], step, 0)


def add_call(labels, front, got):
    lead = front.shape[0]
    n = got.shape[0]
    rows = 32
    return pl.pallas_call(
        add_body,
        out_shape=jax.ShapeDtypeStruct(front.shape, jnp.float32),
        grid_spec=pltpu.PrefetchScalarGridSpec(
            num_scalar_prefetch=1,
            grid=(TILE // rows,),
            in_specs=[
                pl.BlockSpec((lead, rows, TILE), lambda i, _: (0, i, 0)),
                pl.BlockSpec((n, rows, TILE), lambda i, _: (0, i, 0)),
            ],
            out_specs=pl.BlockSpec((lead, rows, TILE), lambda i, _: (0, i, 0)),
        ),
        cost_estimate=pl.CostEstimate(flops=0, bytes_accessed=(n + 2 * lead) * TILE * TILE * 4, transcendentals=0),
    )(labels, front, got)


def split(x):
    high = x.astype(jnp.bfloat16)
    low = (x - high.astype(jnp.float32)).astype(jnp.bfloat16)
    return high, low


def nt(a, b):
    return lax.dot_general(a, b, (((1,), (1,)), ((), ())), preferred_element_type=jnp.float32)


def final_body(col_ref, acc_ref, l_ref, across_ref, out_ref):
    c = col_ref[0]
    t = pl.program_id(0)
    n = across_ref.shape[1]

    @pl.when(c < 4)
    def _():
        at = pl.multiple_of(jnp.minimum(c, 3) * TILE, TILE)
        out_ref[0] = l_ref[:, 0, :, pl.ds(at, TILE)].reshape(TILE, TILE)

    @pl.when((c >= 4) & (t == 0))
    def _():
        out_ref[...] = jnp.zeros_like(out_ref)

    @pl.when((c >= 4) & (t > 0))
    def _():
        ah, al = split(l_ref[...].reshape(TILE, n))
        bh, bl = split(across_ref[...])
        out_ref[0] = acc_ref[0] - (nt(ah, bh) + (nt(ah, bl) + nt(al, bh)))


def final_call(col, acc, gathered, across):
    lead = acc.shape[0]
    j, _, slab, n = gathered.shape
    return pl.pallas_call(
        final_body,
        out_shape=jax.ShapeDtypeStruct(acc.shape, jnp.float32),
        grid_spec=pltpu.PrefetchScalarGridSpec(
            num_scalar_prefetch=1,
            grid=(lead,),
            in_specs=[
                pl.BlockSpec((1, TILE, TILE), lambda i, _: (i, 0, 0)),
                pl.BlockSpec((j, 1, slab, n), lambda i, _: (0, i, 0, 0)),
                pl.BlockSpec((TILE, n), lambda i, _: (0, 0)),
            ],
            out_specs=pl.BlockSpec((1, TILE, TILE), lambda i, _: (i, 0, 0)),
        ),
        compiler_params=pltpu.CompilerParams(vmem_limit_bytes=56 * MIB),
        cost_estimate=pl.CostEstimate(flops=6 * lead * TILE * TILE * n, bytes_accessed=gathered.size * 4, transcendentals=0),
    )(col, acc, gathered, across)


def local(front, child_tiles, child_owner, child_place, child_count, tile_mask):
    n_row = lax.axis_size("row")
    n_col = lax.axis_size("col")
    row_id = lax.axis_index("row")
    col_id = lax.axis_index("col")
    lead = front.shape[0]
    slab = TILE // n_col
    slots = child_tiles.shape[2]
    blocks = front.reshape(lead, TILE, TILE)
    tiles = child_tiles.reshape(slots, TILE, TILE)
    owner = child_owner.reshape(slots)
    place = child_place.reshape(slots)
    count = child_count.reshape(())
    ids = jnp.arange(slots, dtype=jnp.int32)
    hit = owner[None, :] == jnp.arange(n_col, dtype=jnp.int32)[:, None]
    slot_of = jnp.sum(jnp.where(hit, ids[None, :], 0), axis=1)
    label = jnp.sum(jnp.where(hit & (ids < count)[None, :], place[None, :] + 1, 0), axis=1) - 1
    label_f = label.astype(jnp.float32)

    panel_tiles = pack_call(slot_of[:4], tiles)
    slabs = panel_tiles.reshape(4, n_col, slab, TILE).transpose(1, 2, 0, 3).reshape(n_col, slab, 4 * TILE)
    mirrored = blocks[0].T.reshape(n_col, slab, TILE)
    marks = jnp.concatenate(
        [jnp.broadcast_to(label_f[None, :4], (n_col, 4)), label_f[:, None], jnp.zeros((n_col, slab - 5), jnp.float32)], axis=1
    )
    marks = jnp.broadcast_to(marks[:, :, None], (n_col, slab, 128))
    message = jnp.concatenate([slabs, mirrored, marks], axis=2)
    own, parts, got = panel_call(message, lead)

    payload = pack_call(slot_of, tiles)
    if LATE:
        payload, own = lax.optimization_barrier((payload, own))
    arrived = lax.all_to_all(payload, "col", split_axis=0, concat_axis=0, tiled=True)

    row_tiles = jnp.arange(lead, dtype=jnp.int32) * n_row + row_id
    keep = jnp.sum(jnp.where(row_tiles[:, None] == jnp.arange(tile_mask.shape[0])[None, :], tile_mask[None, :], 0), axis=1)
    where = jnp.concatenate([(row_id * TILE + col_id * slab)[None], keep[1:]]).astype(jnp.int32)
    mine = chol_call(where, parts, own)
    gathered, across = rows_call(mine.reshape(lead, slab, 4 * TILE))
    gathered = gathered.reshape(n_col, lead, slab, 4 * TILE)
    across = across.reshape(TILE, 4 * TILE)

    got_labels = got[:, 4, 5 * TILE].astype(jnp.int32)
    acc = add_call(got_labels, blocks, arrived)
    result = final_call(col_id.reshape(1), acc, gathered, across)
    return result.reshape(front.shape)


def solution(mesh):
    return jax.shard_map(
        local,
        mesh=mesh,
        in_specs=(
            P(None, "row", None, None, "col", None),
            P("row", "col", None, None, None),
            P("row", "col", None),
            P("row", "col", None),
            P("row", "col"),
            P(),
        ),
        out_specs=P(None, "row", None, None, "col", None),
        check_vma=False,
    )
```

```python
import jax
import jax.numpy as jnp
from jax import lax
from jax.experimental import pallas as pl
from jax.experimental.pallas import tpu as pltpu
from jax.sharding import PartitionSpec as P

HI = lax.Precision.HIGHEST
NB = 128
SB = 32
TILE = 256
MIB = 1024 * 1024

def dot_nt(a, b):
    return lax.dot_general(a, b, (((1,), (1,)), ((), ())), precision=HI, preferred_element_type=jnp.float32)

def dot_tn(a, b):
    return lax.dot_general(a, b, (((0,), (0,)), ((), ())), precision=HI, preferred_element_type=jnp.float32)

def invert_factor(block):
    sub = lax.broadcasted_iota(jnp.int32, (NB, NB), 0)
    lane = lax.broadcasted_iota(jnp.int32, (NB, NB), 1)
    eye = (sub == lane).astype(jnp.float32)
    rest = jnp.concatenate([block, eye], axis=1)
    done = []
    for sb in range(NB // SB):
        w = rest[:SB]
        rows = []
        for t in range(SB // 8):
            base = sb * SB + t * 8
            h = w.shape[0]
            ids = lax.broadcasted_iota(jnp.int32, (h, NB), 0)
            cols = [jnp.broadcast_to(w[:, base + i:base + i + 1], (h, NB)) for i in range(8)]
            final = []
            for j in range(8):
                cj = cols[j]
                piv = jnp.broadcast_to(cj[j:j + 1], (8, NB))
                rs = lax.rsqrt(piv)
                rs_h = jnp.concatenate([rs] * (h // 8), axis=0)
                inv = rs * rs
                inv_h = jnp.concatenate([inv] * (h // 8), axis=0)
                for i in range(j + 1, 8):
                    ci = jnp.broadcast_to(cj[i:i + 1], (h, NB))
                    cols[i] = cols[i] - cj * (ci * inv_h)
                lj = jnp.where(ids > j, cj * rs_h, 0.0)
                r = w[j:j + 1] * jnp.concatenate([rs[:1], rs[:1]], axis=1)
                final.append(r)
                lw = jnp.concatenate([lj, lj], axis=1)
                w = w - lw * jnp.broadcast_to(r, (h, 2 * NB))
            rows.append(jnp.concatenate(final, axis=0))
            w = w[8:]
        r = jnp.concatenate(rows, axis=0)
        done.append(r[:, NB:])
        if sb + 1 < NB // SB:
            lo = (sb + 1) * SB
            rest = rest[SB:] - dot_tn(r[:, lo:NB], r)
    return jnp.concatenate(done, axis=0)

def load_diag(part_ref, own_ref, where_ref, diag_ref, s):
    n = diag_ref.shape[0]
    m = own_ref.shape[0]
    for q in range(4):
        rows = slice(q * TILE, (q + 1) * TILE)
        diag_ref[rows, :2 * TILE] = part_ref[:, :, :, q].reshape(TILE, 2 * TILE)
        if q >= 2:
            diag_ref[rows, 2 * TILE:] = part_ref[:, :, :, 2 + q].reshape(TILE, 2 * TILE)
    nb = n // NB
    half = nb // 2
    for a in range(nb):
        for b in range(a + 1):
            x = diag_ref[a * NB:(a + 1) * NB, b * NB:(b + 1) * NB]
            if a // half == b // half:
                y = diag_ref[b * NB:(b + 1) * NB, a * NB:(a + 1) * NB]
                x = (x + y.T) * 0.5
            s[a * NB:(a + 1) * NB, b * NB:(b + 1) * NB] = x
        if a + 1 < nb:
            s[a * NB:(a + 1) * NB, (a + 1) * NB:] = jnp.zeros((NB, n - (a + 1) * NB), jnp.float32)
    row0 = lax.axis_index("row") * TILE + lax.axis_index("col") * 8
    s[n:n + 8, :] = s[pl.ds(pl.multiple_of(row0, 8), 8), :]
    for t in range(1, m // 8):
        s[n + 8 * t:n + 8 * t + 8, :] = jnp.where(where_ref[t:t + 1, :1] > 0.0, own_ref[8 * t:8 * t + 8, :], 0.0)
    return row0


def factor_step(s, k):
    n = s.shape[1]
    lo = k * NB
    hi = lo + NB
    inv = invert_factor(s[lo:hi, lo:hi])
    x = dot_nt(s[hi:, lo:hi], inv)
    s[hi:, lo:hi] = x
    at = hi
    while at < n:
        width = NB if at == hi else min(2 * NB, n - at)
        s[at:, at:at + width] = s[at:, at:at + width] - dot_nt(x[at - hi:], x[at - hi:at - hi + width])
        at += width


def split(x):
    high = x.astype(jnp.bfloat16)
    low = (x - high.astype(jnp.float32)).astype(jnp.bfloat16)
    return high, low


def nt(a, b):
    return lax.dot_general(a, b, (((1,), (1,)), ((), ())), preferred_element_type=jnp.float32)


MESH = pl.DeviceIdType.MESH


def here():
    r = lax.axis_index("row")
    c = lax.axis_index("col")
    return r, c, lax.div(c, 8), lax.rem(lax.div(c, 2), 4), lax.rem(c, 2)


def at_col(y, z, k):
    return (y * 4 + z) * 2 + k


def turn(i, d):
    return lax.rem(i + d, 4)


def greet(devices):
    barrier = pltpu.get_barrier_semaphore()
    for device in devices:
        pl.semaphore_signal(barrier, inc=1, device_id=device, device_id_type=MESH)
    pl.semaphore_wait(barrier, len(devices))


def plane_peers(r, y, z, k):
    out = [(r, at_col(y, z, 1 - k))]
    for d in range(1, 4):
        out.append((r, at_col(y, turn(z, d), k)))
        out.append((r, at_col(turn(y, d), z, k)))
    return out


def row_peers(r, c):
    return [(turn(r, d), c) for d in range(1, 4)]


def plane_gather(piece, send, recv, core_send, core_recv, r, y, z, k, early=None, done=None):
    def place(h, a, b):
        return (b, a) if h == 0 else (a, b)

    def axes(h):
        return (z, y) if h == 0 else (y, z)

    def push(h, da, db, to, send_sem, recv_sem):
        a, b = axes(h)
        ref = piece(h, *place(h, turn(a, 4 - da), turn(b, 4 - db)), k)
        copy = pltpu.make_async_remote_copy(
            src_ref=ref, dst_ref=ref, send_sem=send_sem, recv_sem=recv_sem, device_id=to, device_id_type=MESH
        )
        copy.start()
        return copy

    def along_first(h, d):
        a, b = axes(h)
        yy, zz = place(h, turn(a, d), b)
        return push(h, 0, 0, (r, at_col(yy, zz, k)), send.at[h, d, 0], recv.at[h, d, 0])

    def along_second(h, da, d):
        a, b = axes(h)
        yy, zz = place(h, a, turn(b, d))
        return push(h, da, 0, (r, at_col(yy, zz, k)), send.at[h, da, d], recv.at[h, da, d])

    def across(h, da, db):
        return push(h, da, db, (r, at_col(y, z, 1 - k)), core_send.at[h, da, db], core_recv.at[h, da, db])

    first, second, core = {}, {}, {}
    for d in range(1, 4):
        for h in range(2):
            first[h, d] = along_first(h, d)
    for d in range(1, 4):
        for h in range(2):
            second[h, 0, d] = along_second(h, 0, d)
    for h in range(2):
        core[h, 0, 0] = across(h, 0, 0)
    if early is not None:
        early()
    for da in range(1, 4):
        for h in range(2):
            first[h, da].wait_recv()
            for d in range(1, 4):
                second[h, da, d] = along_second(h, da, d)
            core[h, da, 0] = across(h, da, 0)
    for da in range(4):
        for db in range(1, 4):
            for h in range(2):
                second[h, da, db].wait_recv()
                core[h, da, db] = across(h, da, db)
        if done is not None:
            done(da, 0)

    def finish():
        for da in range(4):
            for h in range(2):
                for db in range(4):
                    core[h, da, db].wait_recv()
            if done is not None:
                done(da, 1)
        for group in (first, second, core):
            for copy in group.values():
                copy.wait_send()

    return finish


def gather_sems():
    return [pltpu.SemaphoreType.DMA((2, 4, 4)) for _ in range(4)]


def panel_body(message_ref, own_ref, diag_ref, label_ref, got_ref, share, front, units, packed, msg_send, msg_recv, local_sem,
               f_send, f_recv, u_send, u_recv, send, recv, core_send, core_recv):
    r, c, y, z, k = here()
    n_col = got_ref.shape[0]
    slab = got_ref.shape[1]
    lead = share.shape[1]
    half = units.shape[3]
    greet([(r, lax.rem(c + d, n_col)) for d in range(1, n_col)] + row_peers(r, c))

    def message(d):
        to = lax.rem(c + d, n_col)
        return pltpu.make_async_remote_copy(
            src_ref=message_ref.at[to],
            dst_ref=got_ref.at[c],
            send_sem=msg_send.at[d],
            recv_sem=msg_recv.at[d],
            device_id=(r, to),
            device_id_type=MESH,
        )

    keep = pltpu.make_async_copy(message_ref.at[c], got_ref.at[c], local_sem.at[0])
    keep.start()
    for d in range(1, n_col):
        message(d).start()
    keep.wait()
    for d in range(1, n_col):
        message(d).wait_recv()

    def exchange(src, dst, s_sem, r_sem, d):
        return pltpu.make_async_remote_copy(
            src_ref=src, dst_ref=dst, send_sem=s_sem.at[d], recv_sem=r_sem.at[d], device_id=(turn(r, d), c),
            device_id_type=MESH,
        )

    for q in range(4):
        for t in range(lead):
            share[q, t] = got_ref[4 * t + q, :, 4 * TILE:5 * TILE]
    front[r] = share[r]
    shares = [exchange(share.at[turn(r, d)], front.at[r], f_send, f_recv, d) for d in range(1, 4)]
    for copy in shares:
        copy.start()
    label_ref[...] = got_ref[:, 4, 5 * TILE:5 * TILE + 128]
    own_ref[...] = jnp.zeros_like(own_ref)

    def add(s, carry):
        for q in range(4):
            at = slice(q * TILE, (q + 1) * TILE)
            label = got_ref[s, q:q + 1, 5 * TILE:5 * TILE + 128]
            label = jnp.broadcast_to(jnp.concatenate([label, label], axis=1), (slab, TILE))
            part = got_ref[s, :, at]
            for t in range(lead):
                rows = slice(t * slab, (t + 1) * slab)
                own_ref[rows, at] = own_ref[rows, at] + jnp.where(label == float(t), part, 0.0)
        return carry

    lax.fori_loop(0, n_col, add, 0)
    for copy in shares:
        copy.wait_recv()
    for q in range(4):
        at = slice(q * TILE, (q + 1) * TILE)
        for t in range(lead):
            rows = slice(t * slab, (t + 1) * slab)
            own_ref[rows, at] = own_ref[rows, at] + front[q, t]
    for p in range(2):
        units[r, p] = own_ref[:slab, p * half:(p + 1) * half]
    lines = [exchange(units.at[r], units.at[r], u_send, u_recv, d) for d in range(1, 4)]
    for copy in lines:
        copy.start()
    for copy in lines:
        copy.wait_recv()
    for q in range(4):
        packed[q] = units[q, 0]
    for q in range(2):
        packed[4 + q] = units[2 + q, 1]
    diag_ref[y, z, k] = packed[...]

    def piece(h, yy, zz, kk):
        return diag_ref.at[yy, zz, kk, pl.ds(h * 3, 3)]

    finish = plane_gather(piece, send, recv, core_send, core_recv, r, y, z, k)
    for d in range(1, n_col):
        message(d).wait_send()
    for copy in shares + lines:
        copy.wait_send()
    finish()


def panel_call(message, lead):
    n_col, slab, width = message.shape
    half = 2 * TILE
    dma = pltpu.SemaphoreType.DMA
    vmem = pl.BlockSpec(memory_space=pltpu.VMEM)
    return pl.pallas_call(
        panel_body,
        out_shape=[
            jax.ShapeDtypeStruct((lead * slab, 4 * TILE), jnp.float32),
            jax.ShapeDtypeStruct((4, 4, 2, 6, slab, half), jnp.float32),
            jax.ShapeDtypeStruct((n_col, 128), jnp.float32),
        ],
        in_specs=[vmem],
        out_specs=[vmem] * 3,
        scratch_shapes=[
            pltpu.VMEM((n_col, slab, width), jnp.float32),
            pltpu.VMEM((4, lead, slab, TILE), jnp.float32),
            pltpu.VMEM((4, lead, slab, TILE), jnp.float32),
            pltpu.VMEM((4, 2, slab, half), jnp.float32),
            pltpu.VMEM((6, slab, half), jnp.float32),
            dma((n_col,)),
            dma((n_col,)),
            dma((1,)),
            dma((4,)),
            dma((4,)),
            dma((4,)),
            dma((4,)),
        ]
        + gather_sems(),
        compiler_params=pltpu.CompilerParams(collective_id=0, has_side_effects=True, vmem_limit_bytes=56 * MIB),
        cost_estimate=pl.CostEstimate(flops=0, bytes_accessed=1000, transcendentals=0),
    )(message)


def main_body(keep_ref, label_ref, parts_ref, own_ref, front_ref, payload_ref, out_ref, s, diag, g, across, arrived, high, low,
              a_send, a_recv, local_sem, x_send, x_recv, send, recv, core_send, core_recv):
    r, c, y, z, k = here()
    n_col = arrived.shape[0]
    lead = front_ref.shape[0]
    n = s.shape[1]
    greet([(r, lax.rem(c + d, n_col)) for d in range(1, n_col)] + row_peers(r, c))

    def tile(d):
        to = lax.rem(c + d, n_col)
        return pltpu.make_async_remote_copy(
            src_ref=payload_ref.at[to],
            dst_ref=arrived.at[d],
            send_sem=a_send.at[d],
            recv_sem=a_recv.at[d],
            device_id=(r, to),
            device_id_type=MESH,
        )

    def begin(ds):
        for d in ds:
            @pl.when(lax.rem(c + d, n_col) >= 4)
            def _(d=d):
                tile(d).start()

    own_tile = pltpu.make_async_copy(payload_ref.at[c], arrived.at[0], local_sem.at[0])
    own_tile.start()
    order = list(range(1, n_col))
    plan = [3, 2, 2, 2, 2, 2, 2, 1]
    groups = []
    for size in plan:
        groups.append(order[:size])
        order = order[size:]
    row0 = None
    begin(groups[0])
    row0 = load_diag(parts_ref, own_ref, keep_ref, diag, s)
    for t in range(lead):
        out_ref[t] = front_ref[t]
    for step in range(n // NB):
        if step:
            begin(groups[step])
        factor_step(s, step)
    m = s.shape[0] - n
    ids = lax.broadcasted_iota(jnp.int32, (m, n), 0)
    lane = lax.broadcasted_iota(jnp.int32, (m, n), 1)
    mine = jnp.where((ids >= 8) | (lane <= ids + row0), s[n:, :], 0.0)
    g[y, z, k] = mine.reshape(g.shape[3:])

    half = lead // 2

    def piece(h, yy, zz, kk):
        return g.at[yy, zz, kk, pl.ds(h * half, half)]

    t_of = lax.div(c, 4)
    source = lax.rem(c, 4)
    part = lax.div(t_of, half)

    def cross(h, da, mate, d):
        kk = lax.rem(k + mate, 2)
        if h == 0:
            zz = turn(z, 4 - da)
            src, dst = g.at[:, zz, kk, t_of], across.at[:, zz, kk]
        else:
            yy = turn(y, 4 - da)
            src, dst = g.at[yy, :, kk, t_of], across.at[yy, :, kk]
        return pltpu.make_async_remote_copy(
            src_ref=src, dst_ref=dst, send_sem=x_send.at[mate, da, d], recv_sem=x_recv.at[mate, da],
            device_id=(turn(r, d), c), device_id_type=MESH,
        )

    def forward(da, mate):
        for h in range(2):
            @pl.when((r == source) & (part == h))
            def _(h=h):
                for d in range(1, 4):
                    cross(h, da, mate, d).start()

    later = order

    def early():
        begin(later[:4])

    finish = plane_gather(piece, send, recv, core_send, core_recv, r, y, z, k, early, forward)
    begin(later[4:])

    def absorb(ds):
        @pl.when(c >= 4)
        def _():
            for d in ds:
                if d:
                    tile(d).wait_recv()
            wanted = [
                jnp.concatenate([label_ref[pl.ds(lax.rem(c + n_col - d, n_col), 1), :]] * 2, axis=1) for d in ds
            ]

            def strip(i, carry):
                rows = pl.ds(pl.multiple_of(i * 8, 8), 8)
                acc = [out_ref[t, rows, :] for t in range(lead)]
                for d, want in zip(ds, wanted):
                    part_in = arrived[d, rows, :]
                    want = jnp.broadcast_to(want, (8, TILE))
                    for t in range(lead):
                        acc[t] = acc[t] + jnp.where(want == float(t), part_in, 0.0)
                for t in range(lead):
                    out_ref[t, rows, :] = acc[t]
                return carry

            lax.fori_loop(0, TILE // 8, strip, 0)

    own_tile.wait()
    absorb([0] + sum(groups[:4], []))
    finish()

    @pl.when(r == source)
    def _():
        local_copy = pltpu.make_async_copy(g.at[:, :, :, t_of], across, local_sem.at[1])
        local_copy.start()
        local_copy.wait()

    for h in range(2):
        @pl.when((r != source) & (part == h))
        def _(h=h):
            for mate in range(2):
                for da in range(4):
                    cross(h, da, mate, 1).wait_recv()

    @pl.when(c < 4)
    def _():
        at = pl.multiple_of(jnp.minimum(c, 3) * TILE, TILE)
        for t in range(lead):
            out_ref[t] = g[:, :, :, t, :, pl.ds(at, TILE)].reshape(TILE, TILE)

    @pl.when(c >= 4)
    def _():
        high[...], low[...] = split(across[...].reshape(TILE, n))

        def update(t, carry):
            ah, al = split(g[:, :, :, t].reshape(TILE, n))
            out_ref[t] = out_ref[t] - (nt(ah, high[...]) + (nt(ah, low[...]) + nt(al, high[...])))
            return carry

        lax.fori_loop(1, lead, update, 0)

    absorb(sum(groups[4:], []))
    rest = list(later)
    while rest:
        size = 4 if len(rest) > 6 else 2
        absorb(rest[:size])
        rest = rest[size:]

    @pl.when(c >= 4)
    def _():
        out_ref[0] = jnp.zeros((TILE, TILE), jnp.float32)

    for d in range(1, n_col):
        @pl.when(lax.rem(c + d, n_col) >= 4)
        def _(d=d):
            tile(d).wait_send()

    for h in range(2):
        @pl.when((r == source) & (part == h))
        def _(h=h):
            for mate in range(2):
                for da in range(4):
                    for d in range(1, 4):
                        cross(h, da, mate, d).wait_send()


def main_call(keep, labels, parts, own, blocks, payload):
    lead = blocks.shape[0]
    n_col = payload.shape[0]
    m, n = own.shape
    dma = pltpu.SemaphoreType.DMA
    vmem = pl.BlockSpec(memory_space=pltpu.VMEM)
    return pl.pallas_call(
        main_body,
        out_shape=jax.ShapeDtypeStruct(blocks.shape, jnp.float32),
        in_specs=[vmem] * 5 + [pl.BlockSpec(memory_space=pl.ANY)],
        out_specs=vmem,
        scratch_shapes=[
            pltpu.VMEM((n + m, n), jnp.float32),
            pltpu.VMEM((n, n), jnp.float32),
            pltpu.VMEM((4, 4, 2, lead, m // lead, n), jnp.float32),
            pltpu.VMEM((4, 4, 2, m // lead, n), jnp.float32),
            pltpu.VMEM((n_col, TILE, TILE), jnp.float32),
            pltpu.VMEM((TILE, n), jnp.bfloat16),
            pltpu.VMEM((TILE, n), jnp.bfloat16),
            dma((n_col,)),
            dma((n_col,)),
            dma((2,)),
            dma((2, 4, 4)),
            dma((2, 4)),
        ]
        + gather_sems(),
        compiler_params=pltpu.CompilerParams(collective_id=1, has_side_effects=True, vmem_limit_bytes=58 * MIB),
        cost_estimate=pl.CostEstimate(flops=0, bytes_accessed=1000, transcendentals=0),
    )(keep, labels, parts, own, blocks, payload)


def pack_body(slot_ref, tile_ref, out_ref):
    out_ref[...] = tile_ref[...]


def pack_call(slots, tiles):
    n = slots.shape[0]
    t = tiles.shape[1]
    return pl.pallas_call(
        pack_body,
        out_shape=jax.ShapeDtypeStruct((n, t, t), tiles.dtype),
        grid_spec=pltpu.PrefetchScalarGridSpec(
            num_scalar_prefetch=1,
            grid=(n,),
            in_specs=[pl.BlockSpec((1, t, t), lambda q, slot: (slot[q], 0, 0))],
            out_specs=pl.BlockSpec((1, t, t), lambda q, slot: (q, 0, 0)),
        ),
        cost_estimate=pl.CostEstimate(flops=0, bytes_accessed=n * t * t * 8, transcendentals=0),
    )(slots, tiles)


def local(front, child_tiles, child_owner, child_place, child_count, tile_mask):
    n_row = lax.axis_size("row")
    n_col = lax.axis_size("col")
    row_id = lax.axis_index("row")
    col_id = lax.axis_index("col")
    lead = front.shape[0]
    slab = TILE // n_col
    slots = child_tiles.shape[2]
    blocks = front.reshape(lead, TILE, TILE)
    tiles = child_tiles.reshape(slots, TILE, TILE)
    owner = child_owner.reshape(slots)
    place = child_place.reshape(slots)
    count = child_count.reshape(())
    ids = jnp.arange(slots, dtype=jnp.int32)
    hit = owner[None, :] == jnp.arange(n_col, dtype=jnp.int32)[:, None]
    slot_of = jnp.sum(jnp.where(hit, ids[None, :], 0), axis=1)
    label = jnp.sum(jnp.where(hit & (ids < count)[None, :], place[None, :] + 1, 0), axis=1) - 1
    label_f = label.astype(jnp.float32)

    panel_tiles = pack_call(slot_of[:4], tiles)
    slabs = panel_tiles.reshape(4, n_col, slab, TILE).transpose(1, 2, 0, 3).reshape(n_col, slab, 4 * TILE)
    mirrored = blocks[0].T.reshape(n_col, slab, TILE)
    marks = jnp.concatenate(
        [jnp.broadcast_to(label_f[None, :4], (n_col, 4)), label_f[:, None], jnp.zeros((n_col, slab - 5), jnp.float32)], axis=1
    )
    marks = jnp.broadcast_to(marks[:, :, None], (n_col, slab, 128))
    message = jnp.concatenate([slabs, mirrored, marks], axis=2)
    own, parts, labels = panel_call(message, lead)
    payload = pack_call(slot_of, tiles)
    row_tiles = jnp.arange(lead, dtype=jnp.int32) * n_row + row_id
    keep = jnp.sum(jnp.where(row_tiles[:, None] == jnp.arange(tile_mask.shape[0])[None, :], tile_mask[None, :], 0), axis=1)
    keep = jnp.broadcast_to(keep.astype(jnp.float32)[:, None], (lead, 128))
    result = main_call(keep, labels, parts, own, blocks, payload)
    return result.reshape(front.shape)


def solution(mesh):
    return jax.shard_map(
        local,
        mesh=mesh,
        in_specs=(
            P(None, "row", None, None, "col", None),
            P("row", "col", None, None, None),
            P("row", "col", None),
            P("row", "col", None),
            P("row", "col"),
            P(),
        ),
        out_specs=P(None, "row", None, None, "col", None),
        check_vma=False,
    )
```

```python
import jax
import jax.numpy as jnp
from jax import lax
from jax.experimental import pallas as pl
from jax.experimental.pallas import tpu as pltpu
from jax.sharding import PartitionSpec as P

HI = lax.Precision.HIGHEST
NB = 128
SB = 32
TILE = 256
MIB = 1024 * 1024

def dot_nt(a, b):
    return lax.dot_general(a, b, (((1,), (1,)), ((), ())), precision=HI, preferred_element_type=jnp.float32)

def dot_tn(a, b):
    return lax.dot_general(a, b, (((0,), (0,)), ((), ())), precision=HI, preferred_element_type=jnp.float32)

def invert_factor(block):
    sub = lax.broadcasted_iota(jnp.int32, (NB, NB), 0)
    lane = lax.broadcasted_iota(jnp.int32, (NB, NB), 1)
    eye = (sub == lane).astype(jnp.float32)
    rest = jnp.concatenate([block, eye], axis=1)
    done = []
    for sb in range(NB // SB):
        w = rest[:SB]
        rows = []
        for t in range(SB // 8):
            base = sb * SB + t * 8
            h = w.shape[0]
            ids = lax.broadcasted_iota(jnp.int32, (h, NB), 0)
            cols = [jnp.broadcast_to(w[:, base + i:base + i + 1], (h, NB)) for i in range(8)]
            final = []
            for j in range(8):
                cj = cols[j]
                piv = jnp.broadcast_to(cj[j:j + 1], (8, NB))
                rs = lax.rsqrt(piv)
                rs_h = jnp.concatenate([rs] * (h // 8), axis=0)
                inv = rs * rs
                inv_h = jnp.concatenate([inv] * (h // 8), axis=0)
                for i in range(j + 1, 8):
                    ci = jnp.broadcast_to(cj[i:i + 1], (h, NB))
                    cols[i] = cols[i] - cj * (ci * inv_h)
                lj = jnp.where(ids > j, cj * rs_h, 0.0)
                r = w[j:j + 1] * jnp.concatenate([rs[:1], rs[:1]], axis=1)
                final.append(r)
                lw = jnp.concatenate([lj, lj], axis=1)
                w = w - lw * jnp.broadcast_to(r, (h, 2 * NB))
            rows.append(jnp.concatenate(final, axis=0))
            w = w[8:]
        r = jnp.concatenate(rows, axis=0)
        done.append(r[:, NB:])
        if sb + 1 < NB // SB:
            lo = (sb + 1) * SB
            rest = rest[SB:] - dot_tn(r[:, lo:NB], r)
    return jnp.concatenate(done, axis=0)

def load_diag(part_ref, own_ref, keep_ref, s):
    n = s.shape[1]
    m = own_ref.shape[0]
    nb = n // NB
    half = nb // 2

    def block(a, b):
        unit = a // 2 + (2 if b >= half else 0)
        at = b % half * NB
        y = a % 2 * 2
        return part_ref[y:y + 2, :, :, unit, :, at:at + NB].reshape(NB, NB)

    for a in range(nb):
        for b in range(a + 1):
            x = block(a, b)
            if a // half == b // half:
                x = (x + block(b, a).T) * 0.5
            s[a * NB:(a + 1) * NB, b * NB:(b + 1) * NB] = x
        if a + 1 < nb:
            s[a * NB:(a + 1) * NB, (a + 1) * NB:] = jnp.zeros((NB, n - (a + 1) * NB), jnp.float32)
    row0 = lax.axis_index("row") * TILE + lax.axis_index("col") * 8
    s[n:n + 8, :] = s[pl.ds(pl.multiple_of(row0, 8), 8), :]
    for t in range(1, m // 8):
        s[n + 8 * t:n + 8 * t + 8, :] = jnp.where(keep_ref[t:t + 1, :1] > 0.0, own_ref[8 * t:8 * t + 8, :], 0.0)
    return row0


def factor_step(s, k):
    n = s.shape[1]
    lo = k * NB
    hi = lo + NB
    inv = invert_factor(s[lo:hi, lo:hi])
    x = dot_nt(s[hi:, lo:hi], inv)
    s[hi:, lo:hi] = x
    at = hi
    while at < n:
        width = NB if at == hi else min(2 * NB, n - at)
        s[at:, at:at + width] = s[at:, at:at + width] - dot_nt(x[at - hi:], x[at - hi:at - hi + width])
        at += width


def split(x):
    high = x.astype(jnp.bfloat16)
    low = (x - high.astype(jnp.float32)).astype(jnp.bfloat16)
    return high, low


def nt(a, b):
    return lax.dot_general(a, b, (((1,), (1,)), ((), ())), preferred_element_type=jnp.float32)


MESH = pl.DeviceIdType.MESH


def here():
    r = lax.axis_index("row")
    c = lax.axis_index("col")
    return r, c, lax.div(c, 8), lax.rem(lax.div(c, 2), 4), lax.rem(c, 2)


def at_col(y, z, k):
    return (y * 4 + z) * 2 + k


def turn(i, d):
    return lax.rem(i + d, 4)


def greet(devices):
    barrier = pltpu.get_barrier_semaphore()
    for device in devices:
        pl.semaphore_signal(barrier, inc=1, device_id=device, device_id_type=MESH)
    pl.semaphore_wait(barrier, len(devices))


def plane_peers(r, y, z, k):
    out = [(r, at_col(y, z, 1 - k))]
    for d in range(1, 4):
        out.append((r, at_col(y, turn(z, d), k)))
        out.append((r, at_col(turn(y, d), z, k)))
    return out


def row_peers(r, c):
    return [(turn(r, d), c) for d in range(1, 4)]


def plane_gather(piece, send, recv, core_send, core_recv, r, y, z, k, early=None, done=None):
    def place(h, a, b):
        return (b, a) if h == 0 else (a, b)

    def axes(h):
        return (z, y) if h == 0 else (y, z)

    def push(h, da, db, to, send_sem, recv_sem):
        a, b = axes(h)
        ref = piece(h, *place(h, turn(a, 4 - da), turn(b, 4 - db)), k)
        copy = pltpu.make_async_remote_copy(
            src_ref=ref, dst_ref=ref, send_sem=send_sem, recv_sem=recv_sem, device_id=to, device_id_type=MESH
        )
        copy.start()
        return copy

    def along_first(h, d):
        a, b = axes(h)
        yy, zz = place(h, turn(a, d), b)
        return push(h, 0, 0, (r, at_col(yy, zz, k)), send.at[h, d, 0], recv.at[h, d, 0])

    def along_second(h, da, d):
        a, b = axes(h)
        yy, zz = place(h, a, turn(b, d))
        return push(h, da, 0, (r, at_col(yy, zz, k)), send.at[h, da, d], recv.at[h, da, d])

    def across(h, da, db):
        return push(h, da, db, (r, at_col(y, z, 1 - k)), core_send.at[h, da, db], core_recv.at[h, da, db])

    first, second, core = {}, {}, {}
    for d in range(1, 4):
        for h in range(2):
            first[h, d] = along_first(h, d)
    for d in range(1, 4):
        for h in range(2):
            second[h, 0, d] = along_second(h, 0, d)
    for h in range(2):
        core[h, 0, 0] = across(h, 0, 0)
    if early is not None:
        early()
    for da in range(1, 4):
        for h in range(2):
            first[h, da].wait_recv()
            for d in range(1, 4):
                second[h, da, d] = along_second(h, da, d)
            core[h, da, 0] = across(h, da, 0)
    for da in range(4):
        for db in range(1, 4):
            for h in range(2):
                second[h, da, db].wait_recv()
                core[h, da, db] = across(h, da, db)
        if done is not None:
            done(da, 0)

    def finish():
        for da in range(4):
            for h in range(2):
                for db in range(4):
                    core[h, da, db].wait_recv()
            if done is not None:
                done(da, 1)
        for group in (first, second, core):
            for copy in group.values():
                copy.wait_send()

    return finish


def gather_sems():
    return [pltpu.SemaphoreType.DMA((2, 4, 4)) for _ in range(4)]


MOVES = [(0, 0, 0), (0, 0, 1)]
for group in (
    ((1, 1), (3, 3)),
    ((1, 3), (3, 1)),
    ((1, 0), (3, 0), (0, 1), (0, 3)),
    ((2, 0), (0, 2)),
    ((2, 2),),
    ((2, 1), (2, 3), (1, 2), (3, 2)),
):
    for dk in range(2):
        MOVES += [(dy, dz, dk) for dy, dz in group]
STARTS = {-2: (1, 6), -1: (6, 10), 1: (10, 14), 3: (14, 18), 5: (18, 22)}
EARLY = (22, 24)
LATER = (24, 32)


def main_body(slot_ref, keep_ref, mark_ref, mirror_ref, front_ref, tiles_ref, out_ref, s, parts, own, labels, message, got, payload,
              share, passed, units, g, across, arrived, high, low, m_send, m_recv, f_send, f_recv, u_send, u_recv,
              a_send, a_recv, local_sem, x_send, x_recv, send, recv, core_send, core_recv,
              d_send, d_recv, dcore_send, dcore_recv):
    r, c, y, z, k = here()
    n_col = arrived.shape[0]
    lead = front_ref.shape[0]
    slab = TILE // n_col
    n = s.shape[1]
    peers = [(r, lax.rem(c + d, n_col)) for d in range(1, n_col)] + row_peers(r, c)
    barrier = pltpu.get_barrier_semaphore()
    for device in peers:
        pl.semaphore_signal(barrier, inc=1, device_id=device, device_id_type=MESH)
    for q in range(4):
        message[:, :, q * TILE:(q + 1) * TILE] = tiles_ref[slot_ref[q]].reshape(n_col, slab, TILE)
    message[:, :, 4 * TILE:5 * TILE] = mirror_ref[...]
    message[:, :, 5 * TILE:] = mark_ref[...]
    got[c] = message[c]
    pl.semaphore_wait(barrier, len(peers))

    def letter(d):
        dy, dz, dk = MOVES[d]
        to = at_col(turn(y, dy), turn(z, dz), lax.rem(k + dk, 2))
        return pltpu.make_async_remote_copy(
            src_ref=message.at[to], dst_ref=got.at[c], send_sem=m_send.at[d], recv_sem=m_recv.at[d], device_id=(r, to),
            device_id_type=MESH,
        )

    letters = [letter(d) for d in range(1, n_col)]
    for copy in letters:
        copy.start()
    for q in range(n_col):
        payload[q] = tiles_ref[slot_ref[q]]

    def tile(d):
        dy, dz, dk = MOVES[d]
        to = at_col(turn(y, dy), turn(z, dz), lax.rem(k + dk, 2))
        return to, pltpu.make_async_remote_copy(
            src_ref=payload.at[to],
            dst_ref=arrived.at[d],
            send_sem=a_send.at[d],
            recv_sem=a_recv.at[d],
            device_id=(r, to),
            device_id_type=MESH,
        )

    def begin(ds):
        for d in range(*ds):
            to, copy = tile(d)

            @pl.when(to >= 4)
            def _(copy=copy):
                copy.start()

    begin(STARTS[-2])
    arrived[0] = payload[c]
    for t in range(lead):
        out_ref[t] = front_ref[t]
    for copy in letters:
        copy.wait_recv()

    def exchange(src, dst, s_sem, r_sem, d):
        return pltpu.make_async_remote_copy(
            src_ref=src, dst_ref=dst, send_sem=s_sem.at[d], recv_sem=r_sem.at[d], device_id=(turn(r, d), c),
            device_id_type=MESH,
        )

    for q in range(4):
        for t in range(lead):
            share[q, t] = got[4 * t + q, :, 4 * TILE:5 * TILE]
    passed[r] = share[r]
    shares = [exchange(share.at[turn(r, d)], passed.at[r], f_send, f_recv, d) for d in range(1, 4)]
    for copy in shares:
        copy.start()
    labels[...] = got[:, 4, 5 * TILE:5 * TILE + 128]
    own[...] = jnp.zeros_like(own)

    def add(i, carry):
        for q in range(4):
            at = slice(q * TILE, (q + 1) * TILE)
            acc = [own[t * slab:(t + 1) * slab, at] for t in range(lead)]
            for e in range(8):
                label = got[i * 8 + e, q:q + 1, 5 * TILE:5 * TILE + 128]
                label = jnp.broadcast_to(jnp.concatenate([label, label], axis=1), (slab, TILE))
                part_in = got[i * 8 + e, :, at]
                for t in range(lead):
                    acc[t] = acc[t] + jnp.where(label == float(t), part_in, 0.0)
            for t in range(lead):
                own[t * slab:(t + 1) * slab, at] = acc[t]
        return carry

    lax.fori_loop(0, n_col // 8, add, 0)
    for copy in shares:
        copy.wait_recv()
    for q in range(4):
        at = slice(q * TILE, (q + 1) * TILE)
        for t in range(lead):
            rows = slice(t * slab, (t + 1) * slab)
            own[rows, at] = own[rows, at] + passed[q, t]
    for p in range(2):
        units[r, p] = own[:slab, p * n // 2:(p + 1) * n // 2]
    lines = [exchange(units.at[r], units.at[r], u_send, u_recv, d) for d in range(1, 4)]
    for copy in lines:
        copy.start()
    for copy in lines:
        copy.wait_recv()
    parts[y, z, k] = jnp.concatenate([units[:, 0], units[2:, 1]], axis=0)

    def unit(h, yy, zz, kk):
        return parts.at[yy, zz, kk, pl.ds(h * 3, 3)]

    close = plane_gather(unit, d_send, d_recv, dcore_send, dcore_recv, r, y, z, k)
    begin(STARTS[-1])
    close()
    row0 = load_diag(parts, own, keep_ref, s)
    for step in range(n // NB):
        factor_step(s, step)
        if step in STARTS:
            begin(STARTS[step])
    m = s.shape[0] - n
    ids = lax.broadcasted_iota(jnp.int32, (m, n), 0)
    lane = lax.broadcasted_iota(jnp.int32, (m, n), 1)
    mine = jnp.where((ids >= 8) | (lane <= ids + row0), s[n:, :], 0.0)
    g[y, z, k] = mine.reshape(g.shape[3:])

    half = lead // 2

    def piece(h, yy, zz, kk):
        return g.at[yy, zz, kk, pl.ds(h * half, half)]

    t_of = lax.div(c, 4)
    source = lax.rem(c, 4)
    part = lax.div(t_of, half)

    def cross(h, da, mate, d):
        kk = lax.rem(k + mate, 2)
        if h == 0:
            zz = turn(z, 4 - da)
            src, dst = g.at[:, zz, kk, t_of], across.at[:, zz, kk]
        else:
            yy = turn(y, 4 - da)
            src, dst = g.at[yy, :, kk, t_of], across.at[yy, :, kk]
        return pltpu.make_async_remote_copy(
            src_ref=src, dst_ref=dst, send_sem=x_send.at[mate, da, d], recv_sem=x_recv.at[mate, da],
            device_id=(turn(r, d), c), device_id_type=MESH,
        )

    def forward(da, mate):
        for h in range(2):
            @pl.when((r == source) & (part == h))
            def _(h=h):
                for d in range(1, 4):
                    cross(h, da, mate, d).start()

    def early():
        begin(EARLY)

    finish = plane_gather(piece, send, recv, core_send, core_recv, r, y, z, k, early, forward)
    begin(LATER)

    def absorb(ds):
        @pl.when(c >= 4)
        def _():
            for d in ds:
                if d:
                    tile(d)[1].wait_recv()
            wanted = []
            for d in ds:
                dy, dz, dk = MOVES[d]
                origin = at_col(turn(y, 4 - dy), turn(z, 4 - dz), lax.rem(k + dk, 2))
                wanted.append(jnp.concatenate([labels[pl.ds(origin, 1), :]] * 2, axis=1))

            def strip(i, carry):
                rows = pl.ds(pl.multiple_of(i * 8, 8), 8)
                acc = [out_ref[t, rows, :] for t in range(lead)]
                for d, want in zip(ds, wanted):
                    part_in = arrived[d, rows, :]
                    want = jnp.broadcast_to(want, (8, TILE))
                    for t in range(lead):
                        acc[t] = acc[t] + jnp.where(want == float(t), part_in, 0.0)
                for t in range(lead):
                    out_ref[t, rows, :] = acc[t]
                return carry

            lax.fori_loop(0, TILE // 8, strip, 0)

    absorb(range(0, 10))
    absorb(range(10, 18))
    finish()

    @pl.when(r == source)
    def _():
        local_copy = pltpu.make_async_copy(g.at[:, :, :, t_of], across, local_sem.at[1])
        local_copy.start()
        local_copy.wait()

    for h in range(2):
        @pl.when((r != source) & (part == h))
        def _(h=h):
            for mate in range(2):
                for da in range(4):
                    cross(h, da, mate, 1).wait_recv()

    @pl.when(c < 4)
    def _():
        at = pl.multiple_of(jnp.minimum(c, 3) * TILE, TILE)
        for t in range(lead):
            out_ref[t] = g[:, :, :, t, :, pl.ds(at, TILE)].reshape(TILE, TILE)

    @pl.when(c >= 4)
    def _():
        high[...], low[...] = split(across[...].reshape(TILE, n))

        def update(t, carry):
            ah, al = split(g[:, :, :, t].reshape(TILE, n))
            out_ref[t] = out_ref[t] - (nt(ah, high[...]) + (nt(ah, low[...]) + nt(al, high[...])))
            return carry

        lax.fori_loop(1, lead, update, 0)

    for lo, hi in ((18, 24), (24, 28), (28, 32)):
        absorb(range(lo, hi))

    @pl.when(c >= 4)
    def _():
        out_ref[0] = jnp.zeros((TILE, TILE), jnp.float32)

    for d in range(1, n_col):
        to, copy = tile(d)

        @pl.when(to >= 4)
        def _(copy=copy):
            copy.wait_send()

    for h in range(2):
        @pl.when((r == source) & (part == h))
        def _(h=h):
            for mate in range(2):
                for da in range(4):
                    for d in range(1, 4):
                        cross(h, da, mate, d).wait_send()
    for copy in letters + shares + lines:
        copy.wait_send()


def main_call(slots, keep, marks, mirrored, blocks, tiles):
    lead = blocks.shape[0]
    n_col, slab, _ = mirrored.shape
    n = 4 * TILE
    dma = pltpu.SemaphoreType.DMA
    f32 = jnp.float32
    vmem = pl.BlockSpec(memory_space=pltpu.VMEM)
    return pl.pallas_call(
        main_body,
        out_shape=jax.ShapeDtypeStruct(blocks.shape, f32),
        in_specs=[pl.BlockSpec(memory_space=pltpu.SMEM)] + [vmem] * 5,
        out_specs=vmem,
        scratch_shapes=[
            pltpu.VMEM((n + lead * slab, n), f32),
            pltpu.VMEM((4, 4, 2, 6, slab, n // 2), f32),
            pltpu.VMEM((lead * slab, n), f32),
            pltpu.VMEM((n_col, 128), f32),
            pltpu.VMEM((n_col, slab, 5 * TILE + 128), f32),
            pltpu.VMEM((n_col, slab, 5 * TILE + 128), f32),
            pltpu.VMEM(tiles.shape, f32),
            pltpu.VMEM((4, lead, slab, TILE), f32),
            pltpu.VMEM((4, lead, slab, TILE), f32),
            pltpu.VMEM((4, 2, slab, n // 2), f32),
            pltpu.VMEM((4, 4, 2, lead, slab, n), f32),
            pltpu.VMEM((4, 4, 2, slab, n), f32),
            pltpu.VMEM((n_col, TILE, TILE), f32),
            pltpu.VMEM((TILE, n), jnp.bfloat16),
            pltpu.VMEM((TILE, n), jnp.bfloat16),
            dma((n_col,)),
            dma((n_col,)),
            dma((4,)),
            dma((4,)),
            dma((4,)),
            dma((4,)),
            dma((n_col,)),
            dma((n_col,)),
            dma((2,)),
            dma((2, 4, 4)),
            dma((2, 4)),
        ]
        + gather_sems()
        + gather_sems(),
        compiler_params=pltpu.CompilerParams(collective_id=0, has_side_effects=True, vmem_limit_bytes=60 * MIB),
        cost_estimate=pl.CostEstimate(flops=0, bytes_accessed=1000, transcendentals=0),
    )(slots, keep, marks, mirrored, blocks, tiles)


def local(front, child_tiles, child_owner, child_place, child_count, tile_mask):
    n_row = lax.axis_size("row")
    n_col = lax.axis_size("col")
    row_id = lax.axis_index("row")
    col_id = lax.axis_index("col")
    lead = front.shape[0]
    slab = TILE // n_col
    slots = child_tiles.shape[2]
    blocks = front.reshape(lead, TILE, TILE)
    tiles = child_tiles.reshape(slots, TILE, TILE)
    owner = child_owner.reshape(slots)
    place = child_place.reshape(slots)
    count = child_count.reshape(())
    ids = jnp.arange(slots, dtype=jnp.int32)
    hit = owner[None, :] == jnp.arange(n_col, dtype=jnp.int32)[:, None]
    slot_of = jnp.sum(jnp.where(hit, ids[None, :], 0), axis=1)
    label = jnp.sum(jnp.where(hit & (ids < count)[None, :], place[None, :] + 1, 0), axis=1) - 1
    label_f = label.astype(jnp.float32)

    mirrored = blocks[0].T.reshape(n_col, slab, TILE)
    marks = jnp.concatenate(
        [jnp.broadcast_to(label_f[None, :4], (n_col, 4)), label_f[:, None], jnp.zeros((n_col, slab - 5), jnp.float32)], axis=1
    )
    marks = jnp.broadcast_to(marks[:, :, None], (n_col, slab, 128))
    row_tiles = jnp.arange(lead, dtype=jnp.int32) * n_row + row_id
    keep = jnp.sum(jnp.where(row_tiles[:, None] == jnp.arange(tile_mask.shape[0])[None, :], tile_mask[None, :], 0), axis=1)
    keep = jnp.broadcast_to(keep.astype(jnp.float32)[:, None], (lead, 128))
    result = main_call(slot_of, keep, marks, mirrored, blocks, tiles)
    return result.reshape(front.shape)


def solution(mesh):
    return jax.shard_map(
        local,
        mesh=mesh,
        in_specs=(
            P(None, "row", None, None, "col", None),
            P("row", "col", None, None, None),
            P("row", "col", None),
            P("row", "col", None),
            P("row", "col"),
            P(),
        ),
        out_specs=P(None, "row", None, None, "col", None),
        check_vma=False,
    )
```

```python
import jax
import jax.numpy as jnp
from jax import lax
from jax.experimental import pallas as pl
from jax.experimental.pallas import tpu as pltpu
from jax.sharding import PartitionSpec as P

HI = lax.Precision.HIGHEST
NB = 128
SB = 32
TILE = 256
MIB = 1024 * 1024

def dot_nt(a, b):
    return lax.dot_general(a, b, (((1,), (1,)), ((), ())), precision=HI, preferred_element_type=jnp.float32)

def dot_tn(a, b):
    return lax.dot_general(a, b, (((0,), (0,)), ((), ())), precision=HI, preferred_element_type=jnp.float32)

def invert_factor(block):
    sub = lax.broadcasted_iota(jnp.int32, (NB, NB), 0)
    lane = lax.broadcasted_iota(jnp.int32, (NB, NB), 1)
    eye = (sub == lane).astype(jnp.float32)
    rest = jnp.concatenate([block, eye], axis=1)
    done = []
    for sb in range(NB // SB):
        w = rest[:SB]
        rows = []
        for t in range(SB // 8):
            base = sb * SB + t * 8
            h = w.shape[0]
            ids = lax.broadcasted_iota(jnp.int32, (h, NB), 0)
            cols = [jnp.broadcast_to(w[:, base + i:base + i + 1], (h, NB)) for i in range(8)]
            final = []
            for j in range(8):
                cj = cols[j]
                piv = jnp.broadcast_to(cj[j:j + 1], (8, NB))
                rs = lax.rsqrt(piv)
                rs_h = jnp.concatenate([rs] * (h // 8), axis=0)
                inv = rs * rs
                inv_h = jnp.concatenate([inv] * (h // 8), axis=0)
                for i in range(j + 1, 8):
                    ci = jnp.broadcast_to(cj[i:i + 1], (h, NB))
                    cols[i] = cols[i] - cj * (ci * inv_h)
                lj = jnp.where(ids > j, cj * rs_h, 0.0)
                r = w[j:j + 1] * jnp.concatenate([rs[:1], rs[:1]], axis=1)
                final.append(r)
                lw = jnp.concatenate([lj, lj], axis=1)
                w = w - lw * jnp.broadcast_to(r, (h, 2 * NB))
            rows.append(jnp.concatenate(final, axis=0))
            w = w[8:]
        r = jnp.concatenate(rows, axis=0)
        done.append(r[:, NB:])
        if sb + 1 < NB // SB:
            lo = (sb + 1) * SB
            rest = rest[SB:] - dot_tn(r[:, lo:NB], r)
    return jnp.concatenate(done, axis=0)

def load_diag(left, right, lower, own_ref, mask_ref, s):
    n = s.shape[1]
    m = own_ref.shape[0]
    nb = n // NB
    half = nb // 2

    def block(a, b):
        y = a % 2 * 2
        if b >= half:
            ref, q = lower, a // 2 - 2
        else:
            ref, q = (left, right)[b // 2], a // 2
        at = (b % half if b >= half else b % 2) * NB
        return ref[q, y:y + 2, :, :, :, at:at + NB].reshape(NB, NB)

    for a in range(nb):
        for b in range(a + 1):
            x = block(a, b)
            if a // half == b // half:
                x = (x + block(b, a).T) * 0.5
            s[a * NB:(a + 1) * NB, b * NB:(b + 1) * NB] = x
        if a + 1 < nb:
            s[a * NB:(a + 1) * NB, (a + 1) * NB:] = jnp.zeros((NB, n - (a + 1) * NB), jnp.float32)
    r = lax.axis_index("row")
    row0 = r * TILE + lax.axis_index("col") * 8
    s[n:n + 8, :] = s[pl.ds(pl.multiple_of(row0, 8), 8), :]
    for t in range(1, m // 8):
        s[n + 8 * t:n + 8 * t + 8, :] = jnp.where(mask_ref[4 * t + r] == 1, own_ref[8 * t:8 * t + 8, :], 0.0)
    return row0


def factor_step(s, k):
    n = s.shape[1]
    lo = k * NB
    hi = lo + NB
    inv = invert_factor(s[lo:hi, lo:hi])
    x = dot_nt(s[hi:, lo:hi], inv)
    s[hi:, lo:hi] = x
    at = hi
    while at < n:
        width = NB if at == hi else min(2 * NB, n - at)
        s[at:, at:at + width] = s[at:, at:at + width] - dot_nt(x[at - hi:], x[at - hi:at - hi + width])
        at += width


def split(x):
    high = x.astype(jnp.bfloat16)
    low = (x - high.astype(jnp.float32)).astype(jnp.bfloat16)
    return high, low


def nt(a, b):
    return lax.dot_general(a, b, (((1,), (1,)), ((), ())), preferred_element_type=jnp.float32)


MESH = pl.DeviceIdType.MESH


def here():
    r = lax.axis_index("row")
    c = lax.axis_index("col")
    return r, c, lax.div(c, 8), lax.rem(lax.div(c, 2), 4), lax.rem(c, 2)


def at_col(y, z, k):
    return (y * 4 + z) * 2 + k


def turn(i, d):
    return lax.rem(i + d, 4)


def greet(devices):
    barrier = pltpu.get_barrier_semaphore()
    for device in devices:
        pl.semaphore_signal(barrier, inc=1, device_id=device, device_id_type=MESH)
    pl.semaphore_wait(barrier, len(devices))


def plane_peers(r, y, z, k):
    out = [(r, at_col(y, z, 1 - k))]
    for d in range(1, 4):
        out.append((r, at_col(y, turn(z, d), k)))
        out.append((r, at_col(turn(y, d), z, k)))
    return out


def row_peers(r, c):
    return [(turn(r, d), c) for d in range(1, 4)]


def plane_gather(piece, send, recv, core_send, core_recv, r, y, z, k, early=None, done=None):
    def place(h, a, b):
        return (b, a) if h == 0 else (a, b)

    def axes(h):
        return (z, y) if h == 0 else (y, z)

    def push(h, da, db, to, send_sem, recv_sem):
        a, b = axes(h)
        ref = piece(h, *place(h, turn(a, 4 - da), turn(b, 4 - db)), k)
        copy = pltpu.make_async_remote_copy(
            src_ref=ref, dst_ref=ref, send_sem=send_sem, recv_sem=recv_sem, device_id=to, device_id_type=MESH
        )
        copy.start()
        return copy

    def along_first(h, d):
        a, b = axes(h)
        yy, zz = place(h, turn(a, d), b)
        return push(h, 0, 0, (r, at_col(yy, zz, k)), send.at[h, d, 0], recv.at[h, d, 0])

    def along_second(h, da, d):
        a, b = axes(h)
        yy, zz = place(h, a, turn(b, d))
        return push(h, da, 0, (r, at_col(yy, zz, k)), send.at[h, da, d], recv.at[h, da, d])

    def across(h, da, db):
        return push(h, da, db, (r, at_col(y, z, 1 - k)), core_send.at[h, da, db], core_recv.at[h, da, db])

    first, second, core = {}, {}, {}
    for d in range(1, 4):
        for h in range(2):
            first[h, d] = along_first(h, d)
    for d in range(1, 4):
        for h in range(2):
            second[h, 0, d] = along_second(h, 0, d)
    for h in range(2):
        core[h, 0, 0] = across(h, 0, 0)
    if early is not None:
        early()
    for da in range(1, 4):
        for h in range(2):
            first[h, da].wait_recv()
            for d in range(1, 4):
                second[h, da, d] = along_second(h, da, d)
            core[h, da, 0] = across(h, da, 0)
    for da in range(4):
        for db in range(1, 4):
            for h in range(2):
                second[h, da, db].wait_recv()
                core[h, da, db] = across(h, da, db)
        if done is not None:
            done(da, 0)

    def finish():
        for da in range(4):
            for h in range(2):
                for db in range(4):
                    core[h, da, db].wait_recv()
            if done is not None:
                done(da, 1)
        for group in (first, second, core):
            for copy in group.values():
                copy.wait_send()

    return finish


def gather_sems():
    return [pltpu.SemaphoreType.DMA((2, 4, 4)) for _ in range(4)]


MOVES = [(0, 0, 0), (0, 0, 1)]
for group in (
    ((1, 1), (3, 3)),
    ((1, 3), (3, 1)),
    ((1, 0), (3, 0), (0, 1), (0, 3)),
    ((2, 0), (0, 2)),
    ((2, 2),),
    ((2, 1), (2, 3), (1, 2), (3, 2)),
):
    for dk in range(2):
        MOVES += [(dy, dz, dk) for dy, dz in group]
STARTS = {-2: (1, 6), -1: (6, 10), 1: (10, 14), 3: (14, 18), 5: (18, 22)}
EARLY = (22, 24)
LATER = (24, 32)


def cube_gather(left, right, lower, send, recv, core_send, core_recv, r, y, z, k):
    me = {"x": r, "y": y, "z": z}
    refs = (left, right, lower)
    axes = (("y", "z", "x"), ("z", "x", "y"), ("x", "y", "z"))

    def peer(axis, d):
        at = dict(me)
        at[axis] = turn(at[axis], d)
        return (at["x"], at_col(at["y"], at["z"], k))

    def view(part, last, e):
        at = {}
        for i, axis in enumerate(axes[part]):
            at[axis] = slice(None) if i < last else turn(me[axis], 4 - e) if i == last else me[axis]
        if part == 2:
            at["x"] = slice(None)
        return refs[part].at[at["x"], at["y"], at["z"], k]

    sent = []

    def push(ref, to, s_sem, r_sem):
        copy = pltpu.make_async_remote_copy(
            src_ref=ref, dst_ref=ref, send_sem=s_sem, recv_sem=r_sem, device_id=to, device_id_type=MESH
        )
        copy.start()
        sent.append(copy)
        return copy

    arrive = {}

    def phase(part, p, e):
        ref = view(part, p - 1, e) if p else view(part, 0, 0)
        for d in range(1, 4):
            arrive[part, p, e, d] = push(ref, peer(axes[part][p], d), send.at[part, p, e, d], recv.at[part, p, e, d])

    core = []

    def mate(part, e):
        core.append(push(view(part, 2, e), (r, at_col(y, z, 1 - k)), core_send.at[part, e], core_recv.at[part, e]))

    def corner(d):
        ref = lower.at[r - 2, y, z, k]
        return pltpu.make_async_remote_copy(
            src_ref=ref, dst_ref=ref, send_sem=send.at[2, 0, 0, d], recv_sem=recv.at[2, 0, 0, d], device_id=peer("x", d),
            device_id_type=MESH,
        )

    @pl.when(r >= 2)
    def _():
        for d in range(1, 4):
            corner(d).start()

    for part in range(2):
        phase(part, 0, 0)
    for part in range(2):
        phase(part, 1, 0)
    for e in range(1, 4):
        for part in range(2):
            arrive[part, 0, 0, e].wait_recv()
            phase(part, 1, e)
    for d in range(1, 4):
        @pl.when(turn(r, 4 - d) >= 2)
        def _(d=d):
            ref = lower.at[0, y, z, k]
            pltpu.make_async_remote_copy(
                src_ref=ref, dst_ref=ref, send_sem=send.at[2, 0, 0, d], recv_sem=recv.at[2, 0, 0, d], device_id=peer("x", d),
                device_id_type=MESH,
            ).wait_recv()
    phase(2, 1, 0)
    for part in (2, 0, 1):
        phase(part, 2, 0)
    for e in range(1, 4):
        for part in range(2):
            for f in range(4):
                arrive[part, 1, f, e].wait_recv()
            phase(part, 2, e)
        arrive[2, 1, 0, e].wait_recv()
        phase(2, 2, e)
    for part in range(3):
        mate(part, 0)
    for e in range(1, 4):
        for part in range(3):
            for f in range(4):
                arrive[part, 2, f, e].wait_recv()
            mate(part, e)

    def finish():
        for copy in core:
            copy.wait_recv()
        for copy in sent:
            copy.wait_send()

        @pl.when(r >= 2)
        def _():
            for d in range(1, 4):
                corner(d).wait_send()

    return finish


def main_body(slot_ref, mark_ref, mask_ref, front_ref, child_ref, out_ref, s, left, right, lower, own, labels, message, got, payload,
              tiles_ref, held, share, passed, g, across, arrived, high, low, m_send, m_recv, f_send, f_recv,
              a_send, a_recv, local_sem, x_send, x_recv, send, recv, core_send, core_recv,
              d_send, d_recv, dcore_send, dcore_recv):
    r, c, y, z, k = here()
    n_col = arrived.shape[0]
    lead = out_ref.shape[0]
    slab = TILE // n_col
    n = s.shape[1]
    fetch = pltpu.make_async_copy(front_ref.at[:, 0], held, local_sem.at[0])
    fetch.start()
    fill = pltpu.make_async_copy(child_ref, tiles_ref, local_sem.at[2])
    fill.start()
    peers = [(r, lax.rem(c + d, n_col)) for d in range(1, n_col)] + row_peers(r, c)
    barrier = pltpu.get_barrier_semaphore()
    for device in peers:
        pl.semaphore_signal(barrier, inc=1, device_id=device, device_id_type=MESH)
    sub = lax.broadcasted_iota(jnp.int32, (slab, 128), 0)
    base = jnp.zeros((slab, 128), jnp.float32)
    for q in range(4):
        base = jnp.where(sub == q, mark_ref[q], base)
    for q in range(n_col):
        message[q, :, 5 * TILE:] = jnp.where(sub == 4, mark_ref[q], base)
    fetch.wait()
    message[:, :, 4 * TILE:5 * TILE] = held[:TILE].T.reshape(n_col, slab, TILE)
    fill.wait()
    for q in range(4):
        message[:, :, q * TILE:(q + 1) * TILE] = tiles_ref[slot_ref[q]].reshape(n_col, slab, TILE)
    got[c] = message[c]
    pl.semaphore_wait(barrier, len(peers))

    def letter(d):
        dy, dz, dk = MOVES[d]
        to = at_col(turn(y, dy), turn(z, dz), lax.rem(k + dk, 2))
        return pltpu.make_async_remote_copy(
            src_ref=message.at[to], dst_ref=got.at[c], send_sem=m_send.at[d], recv_sem=m_recv.at[d], device_id=(r, to),
            device_id_type=MESH,
        )

    letters = [letter(d) for d in range(1, n_col)]
    for copy in letters:
        copy.start()
    for q in range(n_col):
        payload[q] = tiles_ref[slot_ref[q]]

    def tile(d):
        dy, dz, dk = MOVES[d]
        to = at_col(turn(y, dy), turn(z, dz), lax.rem(k + dk, 2))
        return to, pltpu.make_async_remote_copy(
            src_ref=payload.at[to],
            dst_ref=arrived.at[d],
            send_sem=a_send.at[d],
            recv_sem=a_recv.at[d],
            device_id=(r, to),
            device_id_type=MESH,
        )

    def begin(ds):
        for d in range(*ds):
            to, copy = tile(d)

            @pl.when(to >= 4)
            def _(copy=copy):
                copy.start()

    begin(STARTS[-2])
    arrived[0] = payload[c]
    for t in range(lead):
        out_ref[t] = held[t * TILE:(t + 1) * TILE]
    for copy in letters:
        copy.wait_recv()

    def exchange(src, dst, s_sem, r_sem, d):
        return pltpu.make_async_remote_copy(
            src_ref=src, dst_ref=dst, send_sem=s_sem.at[d], recv_sem=r_sem.at[d], device_id=(turn(r, d), c),
            device_id_type=MESH,
        )

    for q in range(4):
        for t in range(lead):
            share[q, t] = got[4 * t + q, :, 4 * TILE:5 * TILE]
    passed[r] = share[r]
    shares = [exchange(share.at[turn(r, d)], passed.at[r], f_send, f_recv, d) for d in range(1, 4)]
    for copy in shares:
        copy.start()
    labels[...] = got[:, 4, 5 * TILE:5 * TILE + 128]
    own[...] = jnp.zeros_like(own)

    def add(i, carry):
        for q in range(4):
            at = slice(q * TILE, (q + 1) * TILE)
            acc = [own[t * slab:(t + 1) * slab, at] for t in range(lead)]
            for e in range(8):
                label = got[i * 8 + e, q:q + 1, 5 * TILE:5 * TILE + 128]
                label = jnp.broadcast_to(jnp.concatenate([label, label], axis=1), (slab, TILE))
                part_in = got[i * 8 + e, :, at]
                for t in range(lead):
                    acc[t] = acc[t] + jnp.where(label == float(t), part_in, 0.0)
            for t in range(lead):
                own[t * slab:(t + 1) * slab, at] = acc[t]
        return carry

    lax.fori_loop(0, n_col // 8, add, 0)
    for copy in shares:
        copy.wait_recv()
    for q in range(4):
        at = slice(q * TILE, (q + 1) * TILE)
        for t in range(lead):
            rows = slice(t * slab, (t + 1) * slab)
            own[rows, at] = own[rows, at] + passed[q, t]
    left[r, y, z, k] = own[:slab, :TILE]
    right[r, y, z, k] = own[:slab, TILE:2 * TILE]

    @pl.when(r >= 2)
    def _():
        lower[r - 2, y, z, k] = own[:slab, 2 * TILE:]

    close = cube_gather(left, right, lower, d_send, d_recv, dcore_send, dcore_recv, r, y, z, k)
    begin(STARTS[-1])
    close()
    row0 = load_diag(left, right, lower, own, mask_ref, s)
    for step in range(n // NB):
        factor_step(s, step)
        if step in STARTS:
            begin(STARTS[step])
    m = s.shape[0] - n
    ids = lax.broadcasted_iota(jnp.int32, (m, n), 0)
    lane = lax.broadcasted_iota(jnp.int32, (m, n), 1)
    mine = jnp.where((ids >= 8) | (lane <= ids + row0), s[n:, :], 0.0)
    g[y, z, k] = mine.reshape(g.shape[3:])

    half = lead // 2

    def piece(h, yy, zz, kk):
        return g.at[yy, zz, kk, pl.ds(h * half, half)]

    t_of = lax.div(c, 4)
    source = lax.rem(c, 4)
    part = lax.div(t_of, half)

    def cross(h, da, mate, d):
        kk = lax.rem(k + mate, 2)
        if h == 0:
            zz = turn(z, 4 - da)
            src, dst = g.at[:, zz, kk, t_of], across.at[:, zz, kk]
        else:
            yy = turn(y, 4 - da)
            src, dst = g.at[yy, :, kk, t_of], across.at[yy, :, kk]
        return pltpu.make_async_remote_copy(
            src_ref=src, dst_ref=dst, send_sem=x_send.at[mate, da, d], recv_sem=x_recv.at[mate, da],
            device_id=(turn(r, d), c), device_id_type=MESH,
        )

    def forward(da, mate):
        for h in range(2):
            @pl.when((r == source) & (part == h))
            def _(h=h):
                for d in range(1, 4):
                    cross(h, da, mate, d).start()

    def early():
        begin(EARLY)

    finish = plane_gather(piece, send, recv, core_send, core_recv, r, y, z, k, early, forward)
    begin(LATER)

    def absorb(ds):
        @pl.when(c >= 4)
        def _():
            for d in ds:
                if d:
                    tile(d)[1].wait_recv()
            wanted = []
            for d in ds:
                dy, dz, dk = MOVES[d]
                origin = at_col(turn(y, 4 - dy), turn(z, 4 - dz), lax.rem(k + dk, 2))
                wanted.append(jnp.concatenate([labels[pl.ds(origin, 1), :]] * 2, axis=1))

            def strip(i, carry):
                rows = pl.ds(pl.multiple_of(i * 8, 8), 8)
                acc = [out_ref[t, rows, :] for t in range(lead)]
                for d, want in zip(ds, wanted):
                    part_in = arrived[d, rows, :]
                    want = jnp.broadcast_to(want, (8, TILE))
                    for t in range(lead):
                        acc[t] = acc[t] + jnp.where(want == float(t), part_in, 0.0)
                for t in range(lead):
                    out_ref[t, rows, :] = acc[t]
                return carry

            lax.fori_loop(0, TILE // 8, strip, 0)

    absorb(range(0, 10))
    absorb(range(10, 18))
    finish()

    @pl.when(r == source)
    def _():
        local_copy = pltpu.make_async_copy(g.at[:, :, :, t_of], across, local_sem.at[1])
        local_copy.start()
        local_copy.wait()

    for h in range(2):
        @pl.when((r != source) & (part == h))
        def _(h=h):
            for mate in range(2):
                for da in range(4):
                    cross(h, da, mate, 1).wait_recv()

    @pl.when(c < 4)
    def _():
        at = pl.multiple_of(jnp.minimum(c, 3) * TILE, TILE)
        for t in range(lead):
            out_ref[t] = g[:, :, :, t, :, pl.ds(at, TILE)].reshape(TILE, TILE)

    @pl.when(c >= 4)
    def _():
        high[...], low[...] = split(across[...].reshape(TILE, n))

        def update(t, carry):
            ah, al = split(g[:, :, :, t].reshape(TILE, n))
            out_ref[t] = out_ref[t] - (nt(ah, high[...]) + (nt(ah, low[...]) + nt(al, high[...])))
            return carry

        lax.fori_loop(1, lead, update, 0)

    for lo, hi in ((18, 24), (24, 28), (28, 32)):
        absorb(range(lo, hi))

    @pl.when(c >= 4)
    def _():
        out_ref[0] = jnp.zeros((TILE, TILE), jnp.float32)

    for d in range(1, n_col):
        to, copy = tile(d)

        @pl.when(to >= 4)
        def _(copy=copy):
            copy.wait_send()

    for h in range(2):
        @pl.when((r == source) & (part == h))
        def _(h=h):
            for mate in range(2):
                for da in range(4):
                    for d in range(1, 4):
                        cross(h, da, mate, d).wait_send()
    for copy in letters + shares:
        copy.wait_send()


def main_call(slots, marks, mask, front, tiles):
    n_col = tiles.shape[0]
    slab = TILE // n_col
    n = 4 * TILE
    lead = front.shape[0] // TILE
    dma = pltpu.SemaphoreType.DMA
    f32 = jnp.float32
    smem = pl.BlockSpec(memory_space=pltpu.SMEM)
    return pl.pallas_call(
        main_body,
        out_shape=jax.ShapeDtypeStruct((lead, TILE, TILE), f32),
        in_specs=[smem] * 3 + [pl.BlockSpec(memory_space=pl.ANY)] * 2,
        out_specs=pl.BlockSpec(memory_space=pltpu.VMEM),
        scratch_shapes=[
            pltpu.VMEM((n + lead * slab, n), f32),
            pltpu.VMEM((4, 4, 4, 2, slab, TILE), f32),
            pltpu.VMEM((4, 4, 4, 2, slab, TILE), f32),
            pltpu.VMEM((2, 4, 4, 2, slab, 2 * TILE), f32),
            pltpu.VMEM((lead * slab, n), f32),
            pltpu.VMEM((n_col, 128), f32),
            pltpu.VMEM((n_col, slab, 5 * TILE + 128), f32),
            pltpu.VMEM((n_col, slab, 5 * TILE + 128), f32),
            pltpu.VMEM(tiles.shape, f32),
            pltpu.VMEM(tiles.shape, f32),
            pltpu.VMEM((lead * TILE, TILE), f32),
            pltpu.VMEM((4, lead, slab, TILE), f32),
            pltpu.VMEM((4, lead, slab, TILE), f32),
            pltpu.VMEM((4, 4, 2, lead, slab, n), f32),
            pltpu.VMEM((4, 4, 2, slab, n), f32),
            pltpu.VMEM((n_col, TILE, TILE), f32),
            pltpu.VMEM((TILE, n), jnp.bfloat16),
            pltpu.VMEM((TILE, n), jnp.bfloat16),
            dma((n_col,)),
            dma((n_col,)),
            dma((4,)),
            dma((4,)),
            dma((n_col,)),
            dma((n_col,)),
            dma((3,)),
            dma((2, 4, 4)),
            dma((2, 4)),
        ]
        + gather_sems()
        + [dma((3, 3, 4, 4)), dma((3, 3, 4, 4)), dma((3, 4)), dma((3, 4))],
        compiler_params=pltpu.CompilerParams(collective_id=0, has_side_effects=True, vmem_limit_bytes=60 * MIB),
        cost_estimate=pl.CostEstimate(flops=0, bytes_accessed=1000, transcendentals=0),
    )(slots, marks, mask, front, tiles)


def local(front, child_tiles, child_owner, child_place, child_count, tile_mask):
    n_col = lax.axis_size("col")
    lead = front.shape[0]
    slots = child_tiles.shape[2]
    owner = child_owner.reshape(slots)
    place = child_place.reshape(slots)
    count = child_count.reshape(())
    ids = jnp.arange(slots, dtype=jnp.int32)
    hit = owner[None, :] == jnp.arange(n_col, dtype=jnp.int32)[:, None]
    slot_of = jnp.sum(jnp.where(hit, ids[None, :], 0), axis=1)
    marks = (jnp.sum(jnp.where(hit & (ids < count)[None, :], place[None, :] + 1, 0), axis=1) - 1).astype(jnp.float32)
    result = main_call(slot_of, marks, tile_mask, front.reshape(lead * TILE, 1, TILE), child_tiles.reshape(slots, TILE, TILE))
    return result.reshape(front.shape)


def solution(mesh):
    return jax.shard_map(
        local,
        mesh=mesh,
        in_specs=(
            P(None, "row", None, None, "col", None),
            P("row", "col", None, None, None),
            P("row", "col", None),
            P("row", "col", None),
            P("row", "col"),
            P(),
        ),
        out_specs=P(None, "row", None, None, "col", None),
        check_vma=False,
    )
```

```python
import jax
import jax.numpy as jnp
from jax import lax
from jax.experimental import pallas as pl
from jax.experimental.pallas import tpu as pltpu
from jax.sharding import PartitionSpec as P

HI = lax.Precision.HIGHEST
NB = 128
SB = 32
TILE = 256
MIB = 1024 * 1024

def dot_nt(a, b):
    return lax.dot_general(a, b, (((1,), (1,)), ((), ())), precision=HI, preferred_element_type=jnp.float32)

def dot_tn(a, b):
    return lax.dot_general(a, b, (((0,), (0,)), ((), ())), precision=HI, preferred_element_type=jnp.float32)

def invert_factor(block):
    sub = lax.broadcasted_iota(jnp.int32, (NB, NB), 0)
    lane = lax.broadcasted_iota(jnp.int32, (NB, NB), 1)
    eye = (sub == lane).astype(jnp.float32)
    rest = jnp.concatenate([block, eye], axis=1)
    done = []
    for sb in range(NB // SB):
        w = rest[:SB]
        rows = []
        for t in range(SB // 8):
            base = sb * SB + t * 8
            h = w.shape[0]
            ids = lax.broadcasted_iota(jnp.int32, (h, NB), 0)
            cols = [jnp.broadcast_to(w[:, base + i:base + i + 1], (h, NB)) for i in range(8)]
            final = []
            for j in range(8):
                cj = cols[j]
                piv = jnp.broadcast_to(cj[j:j + 1], (8, NB))
                rs = lax.rsqrt(piv)
                rs_h = jnp.concatenate([rs] * (h // 8), axis=0)
                inv = rs * rs
                inv_h = jnp.concatenate([inv] * (h // 8), axis=0)
                for i in range(j + 1, 8):
                    ci = jnp.broadcast_to(cj[i:i + 1], (h, NB))
                    cols[i] = cols[i] - cj * (ci * inv_h)
                lj = jnp.where(ids > j, cj * rs_h, 0.0)
                r = w[j:j + 1] * jnp.concatenate([rs[:1], rs[:1]], axis=1)
                final.append(r)
                lw = jnp.concatenate([lj, lj], axis=1)
                w = w - lw * jnp.broadcast_to(r, (h, 2 * NB))
            rows.append(jnp.concatenate(final, axis=0))
            w = w[8:]
        r = jnp.concatenate(rows, axis=0)
        done.append(r[:, NB:])
        if sb + 1 < NB // SB:
            lo = (sb + 1) * SB
            rest = rest[SB:] - dot_tn(r[:, lo:NB], r)
    return jnp.concatenate(done, axis=0)

def load_diag(left, right, lower, own_ref, mask_ref, s):
    n = s.shape[1]
    m = own_ref.shape[0]
    nb = n // NB
    half = nb // 2

    def block(a, b):
        y = a % 2 * 2
        if b >= half:
            ref, q = lower, a // 2 - 2
        else:
            ref, q = (left, right)[b // 2], a // 2
        at = (b % half if b >= half else b % 2) * NB
        return ref[q, y:y + 2, :, :, :, at:at + NB].reshape(NB, NB)

    for a in range(nb):
        for b in range(a + 1):
            x = block(a, b)
            if a // half == b // half:
                x = (x + block(b, a).T) * 0.5
            s[a * NB:(a + 1) * NB, b * NB:(b + 1) * NB] = x
        if a + 1 < nb:
            s[a * NB:(a + 1) * NB, (a + 1) * NB:] = jnp.zeros((NB, n - (a + 1) * NB), jnp.float32)
    r = lax.axis_index("row")
    row0 = r * TILE + lax.axis_index("col") * 8
    s[n:n + 8, :] = s[pl.ds(pl.multiple_of(row0, 8), 8), :]
    for t in range(1, m // 8):
        s[n + 8 * t:n + 8 * t + 8, :] = jnp.where(mask_ref[4 * t + r] == 1, own_ref[8 * t:8 * t + 8, :], 0.0)
    return row0


def factor_step(s, k):
    n = s.shape[1]
    lo = k * NB
    hi = lo + NB
    inv = invert_factor(s[lo:hi, lo:hi])
    x = dot_nt(s[hi:, lo:hi], inv)
    s[hi:, lo:hi] = x
    at = hi
    while at < n:
        width = NB if at == hi else min(2 * NB, n - at)
        s[at:, at:at + width] = s[at:, at:at + width] - dot_nt(x[at - hi:], x[at - hi:at - hi + width])
        at += width


def split(x):
    high = x.astype(jnp.bfloat16)
    low = (x - high.astype(jnp.float32)).astype(jnp.bfloat16)
    return high, low


def nt(a, b):
    return lax.dot_general(a, b, (((1,), (1,)), ((), ())), preferred_element_type=jnp.float32)


MESH = pl.DeviceIdType.MESH


def here():
    r = lax.axis_index("row")
    c = lax.axis_index("col")
    return r, c, lax.div(c, 8), lax.rem(lax.div(c, 2), 4), lax.rem(c, 2)


def at_col(y, z, k):
    return (y * 4 + z) * 2 + k


def turn(i, d):
    return lax.rem(i + d, 4)


def greet(devices):
    barrier = pltpu.get_barrier_semaphore()
    for device in devices:
        pl.semaphore_signal(barrier, inc=1, device_id=device, device_id_type=MESH)
    pl.semaphore_wait(barrier, len(devices))


def plane_peers(r, y, z, k):
    out = [(r, at_col(y, z, 1 - k))]
    for d in range(1, 4):
        out.append((r, at_col(y, turn(z, d), k)))
        out.append((r, at_col(turn(y, d), z, k)))
    return out


def row_peers(r, c):
    return [(turn(r, d), c) for d in range(1, 4)]


def plane_gather(piece, send, recv, core_send, core_recv, r, y, z, k, early=None, done=None):
    def place(h, a, b):
        return (b, a) if h == 0 else (a, b)

    def axes(h):
        return (z, y) if h == 0 else (y, z)

    def push(h, da, db, to, send_sem, recv_sem):
        a, b = axes(h)
        ref = piece(h, *place(h, turn(a, 4 - da), turn(b, 4 - db)), k)
        copy = pltpu.make_async_remote_copy(
            src_ref=ref, dst_ref=ref, send_sem=send_sem, recv_sem=recv_sem, device_id=to, device_id_type=MESH
        )
        copy.start()
        return copy

    def along_first(h, d):
        a, b = axes(h)
        yy, zz = place(h, turn(a, d), b)
        return push(h, 0, 0, (r, at_col(yy, zz, k)), send.at[h, d, 0], recv.at[h, d, 0])

    def along_second(h, da, d):
        a, b = axes(h)
        yy, zz = place(h, a, turn(b, d))
        return push(h, da, 0, (r, at_col(yy, zz, k)), send.at[h, da, d], recv.at[h, da, d])

    def across(h, da, db):
        return push(h, da, db, (r, at_col(y, z, 1 - k)), core_send.at[h, da, db], core_recv.at[h, da, db])

    first, second, core = {}, {}, {}
    for d in range(1, 4):
        for h in range(2):
            first[h, d] = along_first(h, d)
    for d in range(1, 4):
        for h in range(2):
            second[h, 0, d] = along_second(h, 0, d)
    for h in range(2):
        core[h, 0, 0] = across(h, 0, 0)
    if early is not None:
        early()
    for da in range(1, 4):
        for h in range(2):
            first[h, da].wait_recv()
            for d in range(1, 4):
                second[h, da, d] = along_second(h, da, d)
            core[h, da, 0] = across(h, da, 0)
    for da in range(4):
        for db in range(1, 4):
            for h in range(2):
                second[h, da, db].wait_recv()
                core[h, da, db] = across(h, da, db)
        if done is not None:
            done(da, 0)

    def finish():
        for da in range(4):
            for h in range(2):
                for db in range(4):
                    core[h, da, db].wait_recv()
            if done is not None:
                done(da, 1)
        for group in (first, second, core):
            for copy in group.values():
                copy.wait_send()

    return finish


def gather_sems():
    return [pltpu.SemaphoreType.DMA((2, 4, 4)) for _ in range(4)]


MOVES = [(0, 0, 0), (0, 0, 1)]
for group in (
    ((1, 1), (3, 3)),
    ((1, 3), (3, 1)),
    ((1, 0), (3, 0), (0, 1), (0, 3)),
    ((2, 0), (0, 2)),
    ((2, 2),),
    ((2, 1), (2, 3), (1, 2), (3, 2)),
):
    for dk in range(2):
        MOVES += [(dy, dz, dk) for dy, dz in group]
STARTS = {-2: (1, 6), -1: (6, 14), 0: (14, 18), 2: (18, 22), 4: (22, 28)}
EARLY = (28, 28)
LATER = (28, 32)


def cube_gather(left, right, lower, send, recv, core_send, core_recv, r, y, z, k):
    me = {"x": r, "y": y, "z": z}
    refs = (left, right, lower)
    axes = (("y", "z", "x"), ("z", "x", "y"), ("x", "y", "z"))

    def peer(axis, d):
        at = dict(me)
        at[axis] = turn(at[axis], d)
        return (at["x"], at_col(at["y"], at["z"], k))

    def view(part, last, e):
        at = {}
        for i, axis in enumerate(axes[part]):
            at[axis] = slice(None) if i < last else turn(me[axis], 4 - e) if i == last else me[axis]
        if part == 2:
            at["x"] = slice(None)
        return refs[part].at[at["x"], at["y"], at["z"], k]

    sent = []

    def push(ref, to, s_sem, r_sem):
        copy = pltpu.make_async_remote_copy(
            src_ref=ref, dst_ref=ref, send_sem=s_sem, recv_sem=r_sem, device_id=to, device_id_type=MESH
        )
        copy.start()
        sent.append(copy)
        return copy

    arrive = {}

    def phase(part, p, e):
        ref = view(part, p - 1, e) if p else view(part, 0, 0)
        for d in range(1, 4):
            arrive[part, p, e, d] = push(ref, peer(axes[part][p], d), send.at[part, p, e, d], recv.at[part, p, e, d])

    core = []

    def mate(part, e):
        core.append(push(view(part, 2, e), (r, at_col(y, z, 1 - k)), core_send.at[part, e], core_recv.at[part, e]))

    def corner(d):
        ref = lower.at[r - 2, y, z, k]
        return pltpu.make_async_remote_copy(
            src_ref=ref, dst_ref=ref, send_sem=send.at[2, 0, 0, d], recv_sem=recv.at[2, 0, 0, d], device_id=peer("x", d),
            device_id_type=MESH,
        )

    @pl.when(r >= 2)
    def _():
        for d in range(1, 4):
            corner(d).start()

    for part in range(2):
        phase(part, 0, 0)
    for part in range(2):
        phase(part, 1, 0)
    for e in range(1, 4):
        for part in range(2):
            arrive[part, 0, 0, e].wait_recv()
            phase(part, 1, e)
    for d in range(1, 4):
        @pl.when(turn(r, 4 - d) >= 2)
        def _(d=d):
            ref = lower.at[0, y, z, k]
            pltpu.make_async_remote_copy(
                src_ref=ref, dst_ref=ref, send_sem=send.at[2, 0, 0, d], recv_sem=recv.at[2, 0, 0, d], device_id=peer("x", d),
                device_id_type=MESH,
            ).wait_recv()
    phase(2, 1, 0)
    for part in (2, 0, 1):
        phase(part, 2, 0)
    for e in range(1, 4):
        for part in range(2):
            for f in range(4):
                arrive[part, 1, f, e].wait_recv()
            phase(part, 2, e)
        arrive[2, 1, 0, e].wait_recv()
        phase(2, 2, e)
    for part in range(3):
        mate(part, 0)
    for e in range(1, 4):
        for part in range(3):
            for f in range(4):
                arrive[part, 2, f, e].wait_recv()
            mate(part, e)

    def finish():
        for copy in core:
            copy.wait_recv()
        for copy in sent:
            copy.wait_send()

        @pl.when(r >= 2)
        def _():
            for d in range(1, 4):
                corner(d).wait_send()

    return finish


def main_body(slot_ref, mark_ref, mask_ref, front_ref, child_ref, out_ref, total, s, left, right, lower, own, labels, message, got, payload,
              tiles_ref, held, share, passed, g, across, arrived, high, low, m_send, m_recv, f_send, f_recv,
              a_send, a_recv, local_sem, o_sem, x_send, x_recv, send, recv, core_send, core_recv,
              d_send, d_recv, dcore_send, dcore_recv):
    r, c, y, z, k = here()
    n_col = arrived.shape[0]
    lead = total.shape[0]
    slab = TILE // n_col
    n = s.shape[1]
    fetch = pltpu.make_async_copy(front_ref.at[:, 0], held, local_sem.at[0])
    fetch.start()
    fill = pltpu.make_async_copy(child_ref, tiles_ref, local_sem.at[2])
    fill.start()
    peers = [(r, lax.rem(c + d, n_col)) for d in range(1, n_col)] + row_peers(r, c)
    barrier = pltpu.get_barrier_semaphore()
    for device in peers:
        pl.semaphore_signal(barrier, inc=1, device_id=device, device_id_type=MESH)
    sub = lax.broadcasted_iota(jnp.int32, (slab, 128), 0)
    base = jnp.zeros((slab, 128), jnp.float32)
    for q in range(4):
        base = jnp.where(sub == q, mark_ref[q], base)
    for q in range(n_col):
        message[q, :, 5 * TILE:] = jnp.where(sub == 4, mark_ref[q], base)
    fetch.wait()
    message[:, :, 4 * TILE:5 * TILE] = held[:TILE].T.reshape(n_col, slab, TILE)
    fill.wait()
    for q in range(4):
        message[:, :, q * TILE:(q + 1) * TILE] = tiles_ref[slot_ref[q]].reshape(n_col, slab, TILE)
    got[c] = message[c]
    pl.semaphore_wait(barrier, len(peers))

    def letter(d):
        dy, dz, dk = MOVES[d]
        to = at_col(turn(y, dy), turn(z, dz), lax.rem(k + dk, 2))
        return pltpu.make_async_remote_copy(
            src_ref=message.at[to], dst_ref=got.at[c], send_sem=m_send.at[d], recv_sem=m_recv.at[d], device_id=(r, to),
            device_id_type=MESH,
        )

    letters = [letter(d) for d in range(1, n_col)]
    for copy in letters:
        copy.start()
    for q in range(n_col):
        payload[q] = tiles_ref[slot_ref[q]]

    def tile(d):
        dy, dz, dk = MOVES[d]
        to = at_col(turn(y, dy), turn(z, dz), lax.rem(k + dk, 2))
        return to, pltpu.make_async_remote_copy(
            src_ref=payload.at[to],
            dst_ref=arrived.at[d],
            send_sem=a_send.at[d],
            recv_sem=a_recv.at[d],
            device_id=(r, to),
            device_id_type=MESH,
        )

    def begin(ds):
        for d in range(*ds):
            to, copy = tile(d)

            @pl.when(to >= 4)
            def _(copy=copy):
                copy.start()

    begin(STARTS[-2])
    arrived[0] = payload[c]
    for t in range(lead):
        total[t] = held[t * TILE:(t + 1) * TILE]
    for copy in letters:
        copy.wait_recv()

    def exchange(src, dst, s_sem, r_sem, d):
        return pltpu.make_async_remote_copy(
            src_ref=src, dst_ref=dst, send_sem=s_sem.at[d], recv_sem=r_sem.at[d], device_id=(turn(r, d), c),
            device_id_type=MESH,
        )

    for q in range(4):
        for t in range(lead):
            share[q, t] = got[4 * t + q, :, 4 * TILE:5 * TILE]
    passed[r] = share[r]
    shares = [exchange(share.at[turn(r, d)], passed.at[r], f_send, f_recv, d) for d in range(1, 4)]
    for copy in shares:
        copy.start()
    labels[...] = got[:, 4, 5 * TILE:5 * TILE + 128]
    own[...] = jnp.zeros_like(own)

    def add(i, carry):
        for q in range(4):
            at = slice(q * TILE, (q + 1) * TILE)
            acc = [own[t * slab:(t + 1) * slab, at] for t in range(lead)]
            for e in range(8):
                label = got[i * 8 + e, q:q + 1, 5 * TILE:5 * TILE + 128]
                label = jnp.broadcast_to(jnp.concatenate([label, label], axis=1), (slab, TILE))
                part_in = got[i * 8 + e, :, at]
                for t in range(lead):
                    acc[t] = acc[t] + jnp.where(label == float(t), part_in, 0.0)
            for t in range(lead):
                own[t * slab:(t + 1) * slab, at] = acc[t]
        return carry

    lax.fori_loop(0, n_col // 8, add, 0)
    for copy in shares:
        copy.wait_recv()
    for q in range(4):
        at = slice(q * TILE, (q + 1) * TILE)
        for t in range(lead):
            rows = slice(t * slab, (t + 1) * slab)
            own[rows, at] = own[rows, at] + passed[q, t]
    left[r, y, z, k] = own[:slab, :TILE]
    right[r, y, z, k] = own[:slab, TILE:2 * TILE]

    @pl.when(r >= 2)
    def _():
        lower[r - 2, y, z, k] = own[:slab, 2 * TILE:]

    close = cube_gather(left, right, lower, d_send, d_recv, dcore_send, dcore_recv, r, y, z, k)
    begin(STARTS[-1])
    close()
    row0 = load_diag(left, right, lower, own, mask_ref, s)
    for step in range(n // NB):
        factor_step(s, step)
        if step in STARTS:
            begin(STARTS[step])
    m = s.shape[0] - n
    ids = lax.broadcasted_iota(jnp.int32, (m, n), 0)
    lane = lax.broadcasted_iota(jnp.int32, (m, n), 1)
    mine = jnp.where((ids >= 8) | (lane <= ids + row0), s[n:, :], 0.0)
    g[y, z, k] = mine.reshape(g.shape[3:])

    half = lead // 2

    def piece(h, yy, zz, kk):
        return g.at[yy, zz, kk, pl.ds(h * half, half)]

    t_of = lax.div(c, 4)
    source = lax.rem(c, 4)
    part = lax.div(t_of, half)

    def cross(h, da, mate, d):
        kk = lax.rem(k + mate, 2)
        if h == 0:
            zz = turn(z, 4 - da)
            src, dst = g.at[:, zz, kk, t_of], across.at[:, zz, kk]
        else:
            yy = turn(y, 4 - da)
            src, dst = g.at[yy, :, kk, t_of], across.at[yy, :, kk]
        return pltpu.make_async_remote_copy(
            src_ref=src, dst_ref=dst, send_sem=x_send.at[mate, da, d], recv_sem=x_recv.at[mate, da],
            device_id=(turn(r, d), c), device_id_type=MESH,
        )

    def forward(da, mate):
        for h in range(2):
            @pl.when((r == source) & (part == h))
            def _(h=h):
                for d in range(1, 4):
                    cross(h, da, mate, d).start()

    def early():
        begin(EARLY)

    finish = plane_gather(piece, send, recv, core_send, core_recv, r, y, z, k, early, forward)
    begin(LATER)

    def absorb(ds):
        @pl.when(c >= 4)
        def _():
            for d in ds:
                if d:
                    tile(d)[1].wait_recv()
            wanted = []
            for d in ds:
                dy, dz, dk = MOVES[d]
                origin = at_col(turn(y, 4 - dy), turn(z, 4 - dz), lax.rem(k + dk, 2))
                wanted.append(jnp.concatenate([labels[pl.ds(origin, 1), :]] * 2, axis=1))

            def strip(i, carry):
                rows = pl.ds(pl.multiple_of(i * 8, 8), 8)
                acc = [total[t, rows, :] for t in range(lead)]
                for d, want in zip(ds, wanted):
                    part_in = arrived[d, rows, :]
                    want = jnp.broadcast_to(want, (8, TILE))
                    for t in range(lead):
                        acc[t] = acc[t] + jnp.where(want == float(t), part_in, 0.0)
                for t in range(lead):
                    total[t, rows, :] = acc[t]
                return carry

            lax.fori_loop(0, TILE // 8, strip, 0)

    absorb(range(0, 10))
    absorb(range(10, 18))
    finish()

    @pl.when(r == source)
    def _():
        local_copy = pltpu.make_async_copy(g.at[:, :, :, t_of], across, local_sem.at[1])
        local_copy.start()
        local_copy.wait()

    for h in range(2):
        @pl.when((r != source) & (part == h))
        def _(h=h):
            for mate in range(2):
                for da in range(4):
                    cross(h, da, mate, 1).wait_recv()

    @pl.when(c < 4)
    def _():
        at = pl.multiple_of(jnp.minimum(c, 3) * TILE, TILE)
        for t in range(lead):
            total[t] = g[:, :, :, t, :, pl.ds(at, TILE)].reshape(TILE, TILE)

    @pl.when(c >= 4)
    def _():
        high[...], low[...] = split(across[...].reshape(TILE, n))

        def update(t, carry):
            ah, al = split(g[:, :, :, t].reshape(TILE, n))
            total[t] = total[t] - (nt(ah, high[...]) + (nt(ah, low[...]) + nt(al, high[...])))
            return carry

        lax.fori_loop(1, lead, update, 0)

    for lo, hi in ((18, 24), (24, 28), (28, 32)):
        absorb(range(lo, hi))

    @pl.when(c >= 4)
    def _():
        total[0] = jnp.zeros((TILE, TILE), jnp.float32)

    stores = [
        pltpu.make_async_copy(total.at[t], out_ref.at[pl.ds(t * TILE, TILE), 0], o_sem.at[t]) for t in range(lead)
    ]
    for copy in stores:
        copy.start()
    for d in range(1, n_col):
        to, copy = tile(d)

        @pl.when(to >= 4)
        def _(copy=copy):
            copy.wait_send()

    for h in range(2):
        @pl.when((r == source) & (part == h))
        def _(h=h):
            for mate in range(2):
                for da in range(4):
                    for d in range(1, 4):
                        cross(h, da, mate, d).wait_send()
    for copy in letters + shares:
        copy.wait_send()
    for copy in stores:
        copy.wait()


def main_call(slots, marks, mask, front, tiles):
    n_col = tiles.shape[0]
    slab = TILE // n_col
    n = 4 * TILE
    lead = front.shape[0] // TILE
    dma = pltpu.SemaphoreType.DMA
    f32 = jnp.float32
    smem = pl.BlockSpec(memory_space=pltpu.SMEM)
    return pl.pallas_call(
        main_body,
        out_shape=jax.ShapeDtypeStruct(front.shape, f32),
        in_specs=[smem] * 3 + [pl.BlockSpec(memory_space=pl.ANY)] * 2,
        out_specs=pl.BlockSpec(memory_space=pl.ANY),
        scratch_shapes=[
            pltpu.VMEM((lead, TILE, TILE), f32),
            pltpu.VMEM((n + lead * slab, n), f32),
            pltpu.VMEM((4, 4, 4, 2, slab, TILE), f32),
            pltpu.VMEM((4, 4, 4, 2, slab, TILE), f32),
            pltpu.VMEM((2, 4, 4, 2, slab, 2 * TILE), f32),
            pltpu.VMEM((lead * slab, n), f32),
            pltpu.VMEM((n_col, 128), f32),
            pltpu.VMEM((n_col, slab, 5 * TILE + 128), f32),
            pltpu.VMEM((n_col, slab, 5 * TILE + 128), f32),
            pltpu.VMEM(tiles.shape, f32),
            pltpu.VMEM(tiles.shape, f32),
            pltpu.VMEM((lead * TILE, TILE), f32),
            pltpu.VMEM((4, lead, slab, TILE), f32),
            pltpu.VMEM((4, lead, slab, TILE), f32),
            pltpu.VMEM((4, 4, 2, lead, slab, n), f32),
            pltpu.VMEM((4, 4, 2, slab, n), f32),
            pltpu.VMEM((n_col, TILE, TILE), f32),
            pltpu.VMEM((TILE, n), jnp.bfloat16),
            pltpu.VMEM((TILE, n), jnp.bfloat16),
            dma((n_col,)),
            dma((n_col,)),
            dma((4,)),
            dma((4,)),
            dma((n_col,)),
            dma((n_col,)),
            dma((3,)),
            dma((lead,)),
            dma((2, 4, 4)),
            dma((2, 4)),
        ]
        + gather_sems()
        + [dma((3, 3, 4, 4)), dma((3, 3, 4, 4)), dma((3, 4)), dma((3, 4))],
        compiler_params=pltpu.CompilerParams(collective_id=0, has_side_effects=True, vmem_limit_bytes=60 * MIB),
        cost_estimate=pl.CostEstimate(flops=0, bytes_accessed=1000, transcendentals=0),
    )(slots, marks, mask, front, tiles)


def local(front, child_tiles, child_owner, child_place, child_count, tile_mask):
    n_col = lax.axis_size("col")
    lead = front.shape[0]
    slots = child_tiles.shape[2]
    owner = child_owner.reshape(slots)
    place = child_place.reshape(slots)
    count = child_count.reshape(())
    ids = jnp.arange(slots, dtype=jnp.int32)
    hit = owner[None, :] == jnp.arange(n_col, dtype=jnp.int32)[:, None]
    slot_of = jnp.sum(jnp.where(hit, ids[None, :], 0), axis=1)
    marks = (jnp.sum(jnp.where(hit & (ids < count)[None, :], place[None, :] + 1, 0), axis=1) - 1).astype(jnp.float32)
    result = main_call(slot_of, marks, tile_mask, front.reshape(lead * TILE, 1, TILE), child_tiles.reshape(slots, TILE, TILE))
    return result.reshape(front.shape)


def solution(mesh):
    return jax.shard_map(
        local,
        mesh=mesh,
        in_specs=(
            P(None, "row", None, None, "col", None),
            P("row", "col", None, None, None),
            P("row", "col", None),
            P("row", "col", None),
            P("row", "col"),
            P(),
        ),
        out_specs=P(None, "row", None, None, "col", None),
        check_vma=False,
    )
```

```python
import jax
import jax.numpy as jnp
from jax import lax
from jax.experimental import pallas as pl
from jax.experimental.pallas import tpu as pltpu
from jax.sharding import PartitionSpec as P

HI = lax.Precision.HIGHEST
NB = 128
SB = 32
TILE = 256
MIB = 1024 * 1024

def dot_nt(a, b):
    return lax.dot_general(a, b, (((1,), (1,)), ((), ())), precision=HI, preferred_element_type=jnp.float32)

def dot_tn(a, b):
    return lax.dot_general(a, b, (((0,), (0,)), ((), ())), precision=HI, preferred_element_type=jnp.float32)

def invert_factor(block):
    sub = lax.broadcasted_iota(jnp.int32, (NB, NB), 0)
    lane = lax.broadcasted_iota(jnp.int32, (NB, NB), 1)
    eye = (sub == lane).astype(jnp.float32)
    rest = jnp.concatenate([block, eye], axis=1)
    done = []
    for sb in range(NB // SB):
        w = rest[:SB]
        rows = []
        for t in range(SB // 8):
            base = sb * SB + t * 8
            h = w.shape[0]
            ids = lax.broadcasted_iota(jnp.int32, (h, NB), 0)
            cols = [jnp.broadcast_to(w[:, base + i:base + i + 1], (h, NB)) for i in range(8)]
            final = []
            for j in range(8):
                cj = cols[j]
                piv = jnp.broadcast_to(cj[j:j + 1], (8, NB))
                rs = lax.rsqrt(piv)
                rs_h = jnp.concatenate([rs] * (h // 8), axis=0)
                inv = rs * rs
                inv_h = jnp.concatenate([inv] * (h // 8), axis=0)
                for i in range(j + 1, 8):
                    ci = jnp.broadcast_to(cj[i:i + 1], (h, NB))
                    cols[i] = cols[i] - cj * (ci * inv_h)
                lj = jnp.where(ids > j, cj * rs_h, 0.0)
                r = w[j:j + 1] * jnp.concatenate([rs[:1], rs[:1]], axis=1)
                final.append(r)
                lw = jnp.concatenate([lj, lj], axis=1)
                w = w - lw * jnp.broadcast_to(r, (h, 2 * NB))
            rows.append(jnp.concatenate(final, axis=0))
            w = w[8:]
        r = jnp.concatenate(rows, axis=0)
        done.append(r[:, NB:])
        if sb + 1 < NB // SB:
            lo = (sb + 1) * SB
            rest = rest[SB:] - dot_tn(r[:, lo:NB], r)
    return jnp.concatenate(done, axis=0)

def load_diag(left, right, lower, own_ref, mask_ref, s):
    n = s.shape[1]
    m = own_ref.shape[0]
    nb = n // NB
    half = nb // 2

    def block(a, b):
        y = a % 2 * 2
        if b >= half:
            ref, q = lower, a // 2 - 2
        else:
            ref, q = (left, right)[b // 2], a // 2
        at = (b % half if b >= half else b % 2) * NB
        return ref[q, y:y + 2, :, :, :, at:at + NB].reshape(NB, NB)

    for a in range(nb):
        for b in range(a + 1):
            x = block(a, b)
            if a // half == b // half:
                x = (x + block(b, a).T) * 0.5
            s[a * NB:(a + 1) * NB, b * NB:(b + 1) * NB] = x
        if a + 1 < nb:
            s[a * NB:(a + 1) * NB, (a + 1) * NB:] = jnp.zeros((NB, n - (a + 1) * NB), jnp.float32)
    r = lax.axis_index("row")
    row0 = r * TILE + lax.axis_index("col") * 8
    s[n:n + 8, :] = s[pl.ds(pl.multiple_of(row0, 8), 8), :]
    for t in range(1, m // 8):
        s[n + 8 * t:n + 8 * t + 8, :] = jnp.where(mask_ref[4 * t + r] == 1, own_ref[8 * t:8 * t + 8, :], 0.0)
    return row0


def factor_step(s, k):
    n = s.shape[1]
    lo = k * NB
    hi = lo + NB
    inv = invert_factor(s[lo:hi, lo:hi])
    x = dot_nt(s[hi:, lo:hi], inv)
    s[hi:, lo:hi] = x
    at = hi
    while at < n:
        width = NB if at == hi else min(2 * NB, n - at)
        s[at:, at:at + width] = s[at:, at:at + width] - dot_nt(x[at - hi:], x[at - hi:at - hi + width])
        at += width


def split(x):
    high = x.astype(jnp.bfloat16)
    low = (x - high.astype(jnp.float32)).astype(jnp.bfloat16)
    return high, low


def nt(a, b):
    return lax.dot_general(a, b, (((1,), (1,)), ((), ())), preferred_element_type=jnp.float32)


MESH = pl.DeviceIdType.MESH


def here():
    r = lax.axis_index("row")
    c = lax.axis_index("col")
    return r, c, lax.div(c, 8), lax.rem(lax.div(c, 2), 4), lax.rem(c, 2)


def at_col(y, z, k):
    return (y * 4 + z) * 2 + k


def turn(i, d):
    return lax.rem(i + d, 4)


def greet(devices):
    barrier = pltpu.get_barrier_semaphore()
    for device in devices:
        pl.semaphore_signal(barrier, inc=1, device_id=device, device_id_type=MESH)
    pl.semaphore_wait(barrier, len(devices))


def plane_peers(r, y, z, k):
    out = [(r, at_col(y, z, 1 - k))]
    for d in range(1, 4):
        out.append((r, at_col(y, turn(z, d), k)))
        out.append((r, at_col(turn(y, d), z, k)))
    return out


def row_peers(r, c):
    return [(turn(r, d), c) for d in range(1, 4)]


def plane_gather(piece, send, recv, core_send, core_recv, r, y, z, k, early=None, done=None):
    def place(h, a, b):
        return (b, a) if h == 0 else (a, b)

    def axes(h):
        return (z, y) if h == 0 else (y, z)

    def push(h, da, db, to, send_sem, recv_sem):
        a, b = axes(h)
        ref = piece(h, *place(h, turn(a, 4 - da), turn(b, 4 - db)), k)
        copy = pltpu.make_async_remote_copy(
            src_ref=ref, dst_ref=ref, send_sem=send_sem, recv_sem=recv_sem, device_id=to, device_id_type=MESH
        )
        copy.start()
        return copy

    def along_first(h, d):
        a, b = axes(h)
        yy, zz = place(h, turn(a, d), b)
        return push(h, 0, 0, (r, at_col(yy, zz, k)), send.at[h, d, 0], recv.at[h, d, 0])

    def along_second(h, da, d):
        a, b = axes(h)
        yy, zz = place(h, a, turn(b, d))
        return push(h, da, 0, (r, at_col(yy, zz, k)), send.at[h, da, d], recv.at[h, da, d])

    def across(h, da, db):
        return push(h, da, db, (r, at_col(y, z, 1 - k)), core_send.at[h, da, db], core_recv.at[h, da, db])

    first, second, core = {}, {}, {}
    for d in range(1, 4):
        for h in range(2):
            first[h, d] = along_first(h, d)
    for d in range(1, 4):
        for h in range(2):
            second[h, 0, d] = along_second(h, 0, d)
    for h in range(2):
        core[h, 0, 0] = across(h, 0, 0)
    if early is not None:
        early()
    for da in range(1, 4):
        for h in range(2):
            first[h, da].wait_recv()
            for d in range(1, 4):
                second[h, da, d] = along_second(h, da, d)
            core[h, da, 0] = across(h, da, 0)
    for da in range(4):
        for db in range(1, 4):
            for h in range(2):
                second[h, da, db].wait_recv()
                core[h, da, db] = across(h, da, db)
        if done is not None:
            done(da, 0)

    def finish():
        for da in range(4):
            for h in range(2):
                for db in range(4):
                    core[h, da, db].wait_recv()
            if done is not None:
                done(da, 1)
        for group in (first, second, core):
            for copy in group.values():
                copy.wait_send()

    return finish


def gather_sems():
    return [pltpu.SemaphoreType.DMA((2, 4, 4)) for _ in range(4)]


MOVES = [(0, 0, 0), (0, 0, 1)]
for group in (
    ((1, 1), (3, 3)),
    ((1, 3), (3, 1)),
    ((1, 0), (3, 0), (0, 1), (0, 3)),
    ((2, 0), (0, 2)),
    ((2, 2),),
    ((2, 1), (2, 3), (1, 2), (3, 2)),
):
    for dk in range(2):
        MOVES += [(dy, dz, dk) for dy, dz in group]
STARTS = {-2: (1, 6), -1: (6, 14), 0: (14, 18), 2: (18, 22), 4: (22, 28)}
EARLY = (28, 28)
LATER = (28, 32)


def cube_gather(left, right, lower, send, recv, core_send, core_recv, r, y, z, k):
    me = {"x": r, "y": y, "z": z}
    refs = (left, right, lower)
    axes = (("y", "z", "x"), ("z", "x", "y"), ("x", "y", "z"))

    def peer(axis, d):
        at = dict(me)
        at[axis] = turn(at[axis], d)
        return (at["x"], at_col(at["y"], at["z"], k))

    def view(part, last, e):
        at = {}
        for i, axis in enumerate(axes[part]):
            at[axis] = slice(None) if i < last else turn(me[axis], 4 - e) if i == last else me[axis]
        if part == 2:
            at["x"] = slice(None)
        return refs[part].at[at["x"], at["y"], at["z"], k]

    sent = []

    def push(ref, to, s_sem, r_sem):
        copy = pltpu.make_async_remote_copy(
            src_ref=ref, dst_ref=ref, send_sem=s_sem, recv_sem=r_sem, device_id=to, device_id_type=MESH
        )
        copy.start()
        sent.append(copy)
        return copy

    arrive = {}

    def phase(part, p, e):
        ref = view(part, p - 1, e) if p else view(part, 0, 0)
        for d in range(1, 4):
            arrive[part, p, e, d] = push(ref, peer(axes[part][p], d), send.at[part, p, e, d], recv.at[part, p, e, d])

    core = []

    def mate(part, e):
        core.append(push(view(part, 2, e), (r, at_col(y, z, 1 - k)), core_send.at[part, e], core_recv.at[part, e]))

    def corner(d):
        ref = lower.at[r - 2, y, z, k]
        return pltpu.make_async_remote_copy(
            src_ref=ref, dst_ref=ref, send_sem=send.at[2, 0, 0, d], recv_sem=recv.at[2, 0, 0, d], device_id=peer("x", d),
            device_id_type=MESH,
        )

    @pl.when(r >= 2)
    def _():
        for d in range(1, 4):
            corner(d).start()

    for part in range(2):
        phase(part, 0, 0)
    for part in range(2):
        phase(part, 1, 0)
    for e in range(1, 4):
        for part in range(2):
            arrive[part, 0, 0, e].wait_recv()
            phase(part, 1, e)
    for d in range(1, 4):
        @pl.when(turn(r, 4 - d) >= 2)
        def _(d=d):
            ref = lower.at[0, y, z, k]
            pltpu.make_async_remote_copy(
                src_ref=ref, dst_ref=ref, send_sem=send.at[2, 0, 0, d], recv_sem=recv.at[2, 0, 0, d], device_id=peer("x", d),
                device_id_type=MESH,
            ).wait_recv()
    phase(2, 1, 0)
    for part in (2, 0, 1):
        phase(part, 2, 0)
    for e in range(1, 4):
        for part in range(2):
            for f in range(4):
                arrive[part, 1, f, e].wait_recv()
            phase(part, 2, e)
        arrive[2, 1, 0, e].wait_recv()
        phase(2, 2, e)
    for part in range(3):
        mate(part, 0)
    for e in range(1, 4):
        for part in range(3):
            for f in range(4):
                arrive[part, 2, f, e].wait_recv()
            mate(part, e)

    def finish():
        for copy in core:
            copy.wait_recv()
        for copy in sent:
            copy.wait_send()

        @pl.when(r >= 2)
        def _():
            for d in range(1, 4):
                corner(d).wait_send()

    return finish


def main_body(slot_ref, mark_ref, mask_ref, front_ref, child_ref, out_ref, s, left, right, lower, own, labels, message, got, payload,
              tiles_ref, held, share, passed, g, across, arrived, high, low, m_send, m_recv, f_send, f_recv,
              a_send, a_recv, local_sem, x_send, x_recv, send, recv, core_send, core_recv,
              d_send, d_recv, dcore_send, dcore_recv):
    r, c, y, z, k = here()
    n_col = arrived.shape[0]
    lead = out_ref.shape[0]
    slab = TILE // n_col
    n = s.shape[1]
    fetch = pltpu.make_async_copy(front_ref.at[:, 0], held, local_sem.at[0])
    fetch.start()
    fill = pltpu.make_async_copy(child_ref, tiles_ref, local_sem.at[2])
    fill.start()
    peers = [(r, lax.rem(c + d, n_col)) for d in range(1, n_col)] + row_peers(r, c)
    barrier = pltpu.get_barrier_semaphore()
    for device in peers:
        pl.semaphore_signal(barrier, inc=1, device_id=device, device_id_type=MESH)
    sub = lax.broadcasted_iota(jnp.int32, (slab, 128), 0)
    base = jnp.zeros((slab, 128), jnp.float32)
    for q in range(4):
        base = jnp.where(sub == q, mark_ref[q], base)
    for q in range(n_col):
        message[q, :, 5 * TILE:] = jnp.where(sub == 4, mark_ref[q], base)
    fetch.wait()
    message[:, :, 4 * TILE:5 * TILE] = held[:TILE].T.reshape(n_col, slab, TILE)
    fill.wait()
    for q in range(4):
        message[:, :, q * TILE:(q + 1) * TILE] = tiles_ref[slot_ref[q]].reshape(n_col, slab, TILE)
    got[c] = message[c]
    pl.semaphore_wait(barrier, len(peers))

    def letter(d):
        dy, dz, dk = MOVES[d]
        to = at_col(turn(y, dy), turn(z, dz), lax.rem(k + dk, 2))
        return pltpu.make_async_remote_copy(
            src_ref=message.at[to], dst_ref=got.at[c], send_sem=m_send.at[d], recv_sem=m_recv.at[d], device_id=(r, to),
            device_id_type=MESH,
        )

    letters = [letter(d) for d in range(1, n_col)]
    for copy in letters:
        copy.start()
    for q in range(n_col):
        payload[q] = tiles_ref[slot_ref[q]]

    def tile(d):
        dy, dz, dk = MOVES[d]
        to = at_col(turn(y, dy), turn(z, dz), lax.rem(k + dk, 2))
        return to, pltpu.make_async_remote_copy(
            src_ref=payload.at[to],
            dst_ref=arrived.at[d],
            send_sem=a_send.at[d],
            recv_sem=a_recv.at[d],
            device_id=(r, to),
            device_id_type=MESH,
        )

    def begin(ds):
        for d in range(*ds):
            to, copy = tile(d)

            @pl.when(to >= 4)
            def _(copy=copy):
                copy.start()

    begin(STARTS[-2])
    arrived[0] = payload[c]
    for t in range(lead):
        out_ref[t] = held[t * TILE:(t + 1) * TILE]
    for copy in letters:
        copy.wait_recv()

    def exchange(src, dst, s_sem, r_sem, d):
        return pltpu.make_async_remote_copy(
            src_ref=src, dst_ref=dst, send_sem=s_sem.at[d], recv_sem=r_sem.at[d], device_id=(turn(r, d), c),
            device_id_type=MESH,
        )

    for q in range(4):
        for t in range(lead):
            share[q, t] = got[4 * t + q, :, 4 * TILE:5 * TILE]
    passed[r] = share[r]
    shares = [exchange(share.at[turn(r, d)], passed.at[r], f_send, f_recv, d) for d in range(1, 4)]
    for copy in shares:
        copy.start()
    labels[...] = got[:, 4, 5 * TILE:5 * TILE + 128]
    own[...] = jnp.zeros_like(own)

    def add(i, carry):
        for q in range(4):
            at = slice(q * TILE, (q + 1) * TILE)
            acc = [own[t * slab:(t + 1) * slab, at] for t in range(lead)]
            for e in range(8):
                label = got[i * 8 + e, q:q + 1, 5 * TILE:5 * TILE + 128]
                label = jnp.broadcast_to(jnp.concatenate([label, label], axis=1), (slab, TILE))
                part_in = got[i * 8 + e, :, at]
                for t in range(lead):
                    acc[t] = acc[t] + jnp.where(label == float(t), part_in, 0.0)
            for t in range(lead):
                own[t * slab:(t + 1) * slab, at] = acc[t]
        return carry

    lax.fori_loop(0, n_col // 8, add, 0)
    for copy in shares:
        copy.wait_recv()
    for q in range(4):
        at = slice(q * TILE, (q + 1) * TILE)
        for t in range(lead):
            rows = slice(t * slab, (t + 1) * slab)
            own[rows, at] = own[rows, at] + passed[q, t]
    left[r, y, z, k] = own[:slab, :TILE]
    right[r, y, z, k] = own[:slab, TILE:2 * TILE]

    @pl.when(r >= 2)
    def _():
        lower[r - 2, y, z, k] = own[:slab, 2 * TILE:]

    close = cube_gather(left, right, lower, d_send, d_recv, dcore_send, dcore_recv, r, y, z, k)
    begin(STARTS[-1])
    close()
    row0 = load_diag(left, right, lower, own, mask_ref, s)
    for step in range(n // NB):
        factor_step(s, step)
        if step in STARTS:
            begin(STARTS[step])
    m = s.shape[0] - n
    ids = lax.broadcasted_iota(jnp.int32, (m, n), 0)
    lane = lax.broadcasted_iota(jnp.int32, (m, n), 1)
    mine = jnp.where((ids >= 8) | (lane <= ids + row0), s[n:, :], 0.0)
    g[y, z, k] = mine.reshape(g.shape[3:])

    half = lead // 2

    def piece(h, yy, zz, kk):
        return g.at[yy, zz, kk, pl.ds(h * half, half)]

    t_of = lax.div(c, 4)
    source = lax.rem(c, 4)
    part = lax.div(t_of, half)

    def cross(h, da, mate, d):
        kk = lax.rem(k + mate, 2)
        if h == 0:
            zz = turn(z, 4 - da)
            src, dst = g.at[:, zz, kk, t_of], across.at[:, zz, kk]
        else:
            yy = turn(y, 4 - da)
            src, dst = g.at[yy, :, kk, t_of], across.at[yy, :, kk]
        return pltpu.make_async_remote_copy(
            src_ref=src, dst_ref=dst, send_sem=x_send.at[mate, da, d], recv_sem=x_recv.at[mate, da],
            device_id=(turn(r, d), c), device_id_type=MESH,
        )

    def forward(da, mate):
        for h in range(2):
            @pl.when((r == source) & (part == h))
            def _(h=h):
                for d in range(1, 4):
                    cross(h, da, mate, d).start()

    def early():
        begin(EARLY)

    finish = plane_gather(piece, send, recv, core_send, core_recv, r, y, z, k, early, forward)
    begin(LATER)

    def absorb(ds):
        @pl.when(c >= 4)
        def _():
            for d in ds:
                if d:
                    tile(d)[1].wait_recv()
            wanted = []
            for d in ds:
                dy, dz, dk = MOVES[d]
                origin = at_col(turn(y, 4 - dy), turn(z, 4 - dz), lax.rem(k + dk, 2))
                wanted.append(jnp.concatenate([labels[pl.ds(origin, 1), :]] * 2, axis=1))

            def strip(i, carry):
                rows = pl.ds(pl.multiple_of(i * 8, 8), 8)
                acc = [out_ref[t, rows, :] for t in range(lead)]
                for d, want in zip(ds, wanted):
                    part_in = arrived[d, rows, :]
                    want = jnp.broadcast_to(want, (8, TILE))
                    for t in range(lead):
                        acc[t] = acc[t] + jnp.where(want == float(t), part_in, 0.0)
                for t in range(lead):
                    out_ref[t, rows, :] = acc[t]
                return carry

            lax.fori_loop(0, TILE // 8, strip, 0)

    absorb(range(0, 10))
    absorb(range(10, 18))
    finish()

    @pl.when(r == source)
    def _():
        local_copy = pltpu.make_async_copy(g.at[:, :, :, t_of], across, local_sem.at[1])
        local_copy.start()
        local_copy.wait()

    for h in range(2):
        @pl.when((r != source) & (part == h))
        def _(h=h):
            for mate in range(2):
                for da in range(4):
                    cross(h, da, mate, 1).wait_recv()

    @pl.when(c < 4)
    def _():
        at = pl.multiple_of(jnp.minimum(c, 3) * TILE, TILE)
        for t in range(lead):
            out_ref[t] = g[:, :, :, t, :, pl.ds(at, TILE)].reshape(TILE, TILE)

    @pl.when(c >= 4)
    def _():
        high[...], low[...] = split(across[...].reshape(TILE, n))

        def update(t, carry):
            ah, al = split(g[:, :, :, t].reshape(TILE, n))
            out_ref[t] = out_ref[t] - (nt(ah, high[...]) + (nt(ah, low[...]) + nt(al, high[...])))
            return carry

        lax.fori_loop(1, lead, update, 0)

    for lo, hi in ((18, 24), (24, 28), (28, 32)):
        absorb(range(lo, hi))

    @pl.when(c >= 4)
    def _():
        out_ref[0] = jnp.zeros((TILE, TILE), jnp.float32)

    for d in range(1, n_col):
        to, copy = tile(d)

        @pl.when(to >= 4)
        def _(copy=copy):
            copy.wait_send()

    for h in range(2):
        @pl.when((r == source) & (part == h))
        def _(h=h):
            for mate in range(2):
                for da in range(4):
                    for d in range(1, 4):
                        cross(h, da, mate, d).wait_send()
    for copy in letters + shares:
        copy.wait_send()


def main_call(slots, marks, mask, front, tiles):
    n_col = tiles.shape[0]
    slab = TILE // n_col
    n = 4 * TILE
    lead = front.shape[0] // TILE
    dma = pltpu.SemaphoreType.DMA
    f32 = jnp.float32
    smem = pl.BlockSpec(memory_space=pltpu.SMEM)
    return pl.pallas_call(
        main_body,
        out_shape=jax.ShapeDtypeStruct((lead, TILE, TILE), f32),
        in_specs=[smem] * 3 + [pl.BlockSpec(memory_space=pl.ANY)] * 2,
        out_specs=pl.BlockSpec(memory_space=pltpu.VMEM),
        scratch_shapes=[
            pltpu.VMEM((n + lead * slab, n), f32),
            pltpu.VMEM((4, 4, 4, 2, slab, TILE), f32),
            pltpu.VMEM((4, 4, 4, 2, slab, TILE), f32),
            pltpu.VMEM((2, 4, 4, 2, slab, 2 * TILE), f32),
            pltpu.VMEM((lead * slab, n), f32),
            pltpu.VMEM((n_col, 128), f32),
            pltpu.VMEM((n_col, slab, 5 * TILE + 128), f32),
            pltpu.VMEM((n_col, slab, 5 * TILE + 128), f32),
            pltpu.VMEM(tiles.shape, f32),
            pltpu.VMEM(tiles.shape, f32),
            pltpu.VMEM((lead * TILE, TILE), f32),
            pltpu.VMEM((4, lead, slab, TILE), f32),
            pltpu.VMEM((4, lead, slab, TILE), f32),
            pltpu.VMEM((4, 4, 2, lead, slab, n), f32),
            pltpu.VMEM((4, 4, 2, slab, n), f32),
            pltpu.VMEM((n_col, TILE, TILE), f32),
            pltpu.VMEM((TILE, n), jnp.bfloat16),
            pltpu.VMEM((TILE, n), jnp.bfloat16),
            dma((n_col,)),
            dma((n_col,)),
            dma((4,)),
            dma((4,)),
            dma((n_col,)),
            dma((n_col,)),
            dma((3,)),
            dma((2, 4, 4)),
            dma((2, 4)),
        ]
        + gather_sems()
        + [dma((3, 3, 4, 4)), dma((3, 3, 4, 4)), dma((3, 4)), dma((3, 4))],
        compiler_params=pltpu.CompilerParams(collective_id=0, has_side_effects=True, vmem_limit_bytes=60 * MIB),
        cost_estimate=pl.CostEstimate(flops=0, bytes_accessed=1000, transcendentals=0),
    )(slots, marks, mask, front, tiles)


def store_body(in_ref, out_ref, sem):
    copies = [
        pltpu.make_async_copy(in_ref.at[t], out_ref.at[pl.ds(t * TILE, TILE), 0], sem.at[t]) for t in range(in_ref.shape[0])
    ]
    for copy in copies:
        copy.start()
    for copy in copies:
        copy.wait()


def store_call(x):
    lead = x.shape[0]
    spec = pl.BlockSpec(memory_space=pl.ANY)
    return pl.pallas_call(
        store_body,
        out_shape=jax.ShapeDtypeStruct((lead * TILE, 1, TILE), x.dtype),
        in_specs=[spec],
        out_specs=spec,
        scratch_shapes=[pltpu.SemaphoreType.DMA((lead,))],
    )(x)


def local(front, child_tiles, child_owner, child_place, child_count, tile_mask):
    n_col = lax.axis_size("col")
    lead = front.shape[0]
    slots = child_tiles.shape[2]
    owner = child_owner.reshape(slots)
    place = child_place.reshape(slots)
    count = child_count.reshape(())
    ids = jnp.arange(slots, dtype=jnp.int32)
    hit = owner[None, :] == jnp.arange(n_col, dtype=jnp.int32)[:, None]
    slot_of = jnp.sum(jnp.where(hit, ids[None, :], 0), axis=1)
    marks = (jnp.sum(jnp.where(hit & (ids < count)[None, :], place[None, :] + 1, 0), axis=1) - 1).astype(jnp.float32)
    result = main_call(slot_of, marks, tile_mask, front.reshape(lead * TILE, 1, TILE), child_tiles.reshape(slots, TILE, TILE))
    return store_call(result).reshape(front.shape)


def solution(mesh):
    return jax.shard_map(
        local,
        mesh=mesh,
        in_specs=(
            P(None, "row", None, None, "col", None),
            P("row", "col", None, None, None),
            P("row", "col", None),
            P("row", "col", None),
            P("row", "col"),
            P(),
        ),
        out_specs=P(None, "row", None, None, "col", None),
        check_vma=False,
    )
```

```python
import jax
import jax.numpy as jnp
from jax import lax
from jax.experimental import pallas as pl
from jax.experimental.pallas import tpu as pltpu
from jax.sharding import PartitionSpec as P

HI = lax.Precision.HIGHEST
NB = 128
SB = 32
TILE = 256
MIB = 1024 * 1024

def dot_nt(a, b):
    return lax.dot_general(a, b, (((1,), (1,)), ((), ())), precision=HI, preferred_element_type=jnp.float32)

def dot_tn(a, b):
    return lax.dot_general(a, b, (((0,), (0,)), ((), ())), precision=HI, preferred_element_type=jnp.float32)

def invert_factor(block):
    sub = lax.broadcasted_iota(jnp.int32, (NB, NB), 0)
    lane = lax.broadcasted_iota(jnp.int32, (NB, NB), 1)
    eye = (sub == lane).astype(jnp.float32)
    rest = jnp.concatenate([block, eye], axis=1)
    done = []
    for sb in range(NB // SB):
        w = rest[:SB]
        rows = []
        for t in range(SB // 8):
            base = sb * SB + t * 8
            h = w.shape[0]
            ids = lax.broadcasted_iota(jnp.int32, (h, NB), 0)
            cols = [jnp.broadcast_to(w[:, base + i:base + i + 1], (h, NB)) for i in range(8)]
            final = []
            for j in range(8):
                cj = cols[j]
                piv = jnp.broadcast_to(cj[j:j + 1], (8, NB))
                rs = lax.rsqrt(piv)
                rs_h = jnp.concatenate([rs] * (h // 8), axis=0)
                inv = rs * rs
                inv_h = jnp.concatenate([inv] * (h // 8), axis=0)
                for i in range(j + 1, 8):
                    ci = jnp.broadcast_to(cj[i:i + 1], (h, NB))
                    cols[i] = cols[i] - cj * (ci * inv_h)
                lj = jnp.where(ids > j, cj * rs_h, 0.0)
                r = w[j:j + 1] * jnp.concatenate([rs[:1], rs[:1]], axis=1)
                final.append(r)
                lw = jnp.concatenate([lj, lj], axis=1)
                w = w - lw * jnp.broadcast_to(r, (h, 2 * NB))
            rows.append(jnp.concatenate(final, axis=0))
            w = w[8:]
        r = jnp.concatenate(rows, axis=0)
        done.append(r[:, NB:])
        if sb + 1 < NB // SB:
            lo = (sb + 1) * SB
            rest = rest[SB:] - dot_tn(r[:, lo:NB], r)
    return jnp.concatenate(done, axis=0)

def load_diag(left, right, lower, own_ref, mask_ref, s):
    n = s.shape[1]
    m = own_ref.shape[0]
    nb = n // NB
    half = nb // 2

    def block(a, b):
        y = a % 2 * 2
        if b >= half:
            ref, q = lower, a // 2 - 2
        else:
            ref, q = (left, right)[b // 2], a // 2
        at = (b % half if b >= half else b % 2) * NB
        return ref[q, y:y + 2, :, :, :, at:at + NB].reshape(NB, NB)

    for a in range(nb):
        for b in range(a + 1):
            x = block(a, b)
            if a // half == b // half:
                x = (x + block(b, a).T) * 0.5
            s[a * NB:(a + 1) * NB, b * NB:(b + 1) * NB] = x
        if a + 1 < nb:
            s[a * NB:(a + 1) * NB, (a + 1) * NB:] = jnp.zeros((NB, n - (a + 1) * NB), jnp.float32)
    r = lax.axis_index("row")
    row0 = r * TILE + lax.axis_index("col") * 8
    s[n:n + 8, :] = s[pl.ds(pl.multiple_of(row0, 8), 8), :]
    for t in range(1, m // 8):
        s[n + 8 * t:n + 8 * t + 8, :] = jnp.where(mask_ref[4 * t + r] == 1, own_ref[8 * t:8 * t + 8, :], 0.0)
    return row0


def factor_step(s, k):
    n = s.shape[1]
    lo = k * NB
    hi = lo + NB
    inv = invert_factor(s[lo:hi, lo:hi])
    x = dot_nt(s[hi:, lo:hi], inv)
    s[hi:, lo:hi] = x
    at = hi
    while at < n:
        width = NB if at == hi else min(2 * NB, n - at)
        s[at:, at:at + width] = s[at:, at:at + width] - dot_nt(x[at - hi:], x[at - hi:at - hi + width])
        at += width


def split(x):
    high = x.astype(jnp.bfloat16)
    low = (x - high.astype(jnp.float32)).astype(jnp.bfloat16)
    return high, low


def nt(a, b):
    return lax.dot_general(a, b, (((1,), (1,)), ((), ())), preferred_element_type=jnp.float32)


MESH = pl.DeviceIdType.MESH


def here():
    r = lax.axis_index("row")
    c = lax.axis_index("col")
    return r, c, lax.div(c, 8), lax.rem(lax.div(c, 2), 4), lax.rem(c, 2)


def at_col(y, z, k):
    return (y * 4 + z) * 2 + k


def turn(i, d):
    return lax.rem(i + d, 4)


def greet(devices):
    barrier = pltpu.get_barrier_semaphore()
    for device in devices:
        pl.semaphore_signal(barrier, inc=1, device_id=device, device_id_type=MESH)
    pl.semaphore_wait(barrier, len(devices))


def plane_peers(r, y, z, k):
    out = [(r, at_col(y, z, 1 - k))]
    for d in range(1, 4):
        out.append((r, at_col(y, turn(z, d), k)))
        out.append((r, at_col(turn(y, d), z, k)))
    return out


def row_peers(r, c):
    return [(turn(r, d), c) for d in range(1, 4)]


def plane_gather(piece, send, recv, core_send, core_recv, r, y, z, k, early=None, done=None):
    def place(h, a, b):
        return (b, a) if h == 0 else (a, b)

    def axes(h):
        return (z, y) if h == 0 else (y, z)

    def push(h, da, db, to, send_sem, recv_sem):
        a, b = axes(h)
        ref = piece(h, *place(h, turn(a, 4 - da), turn(b, 4 - db)), k)
        copy = pltpu.make_async_remote_copy(
            src_ref=ref, dst_ref=ref, send_sem=send_sem, recv_sem=recv_sem, device_id=to, device_id_type=MESH
        )
        copy.start()
        return copy

    def along_first(h, d):
        a, b = axes(h)
        yy, zz = place(h, turn(a, d), b)
        return push(h, 0, 0, (r, at_col(yy, zz, k)), send.at[h, d, 0], recv.at[h, d, 0])

    def along_second(h, da, d):
        a, b = axes(h)
        yy, zz = place(h, a, turn(b, d))
        return push(h, da, 0, (r, at_col(yy, zz, k)), send.at[h, da, d], recv.at[h, da, d])

    def across(h, da, db):
        return push(h, da, db, (r, at_col(y, z, 1 - k)), core_send.at[h, da, db], core_recv.at[h, da, db])

    first, second, core = {}, {}, {}
    for d in range(1, 4):
        for h in range(2):
            first[h, d] = along_first(h, d)
    for d in range(1, 4):
        for h in range(2):
            second[h, 0, d] = along_second(h, 0, d)
    for h in range(2):
        core[h, 0, 0] = across(h, 0, 0)
    if early is not None:
        early()
    for da in range(1, 4):
        for h in range(2):
            first[h, da].wait_recv()
            for d in range(1, 4):
                second[h, da, d] = along_second(h, da, d)
            core[h, da, 0] = across(h, da, 0)
    for da in range(4):
        for db in range(1, 4):
            for h in range(2):
                second[h, da, db].wait_recv()
                core[h, da, db] = across(h, da, db)
        if done is not None:
            done(da, 0)

    def finish():
        for da in range(4):
            for h in range(2):
                for db in range(4):
                    core[h, da, db].wait_recv()
            if done is not None:
                done(da, 1)
        for group in (first, second, core):
            for copy in group.values():
                copy.wait_send()

    return finish


def gather_sems():
    return [pltpu.SemaphoreType.DMA((2, 4, 4)) for _ in range(4)]


MOVES = [(0, 0, 0), (0, 0, 1)]
for group in (
    ((1, 1), (3, 3)),
    ((1, 3), (3, 1)),
    ((1, 0), (3, 0), (0, 1), (0, 3)),
    ((2, 0), (0, 2)),
    ((2, 2),),
    ((2, 1), (2, 3), (1, 2), (3, 2)),
):
    for dk in range(2):
        MOVES += [(dy, dz, dk) for dy, dz in group]
STARTS = {-2: (1, 6), -1: (6, 14), 0: (14, 18), 2: (18, 22), 4: (22, 28)}
EARLY = (28, 28)
LATER = (28, 32)


def cube_gather(left, right, lower, send, recv, core_send, core_recv, r, y, z, k):
    me = {"x": r, "y": y, "z": z}
    refs = (left, right, lower)
    axes = (("y", "z", "x"), ("z", "x", "y"), ("x", "y", "z"))

    def peer(axis, d):
        at = dict(me)
        at[axis] = turn(at[axis], d)
        return (at["x"], at_col(at["y"], at["z"], k))

    def view(part, last, e):
        at = {}
        for i, axis in enumerate(axes[part]):
            at[axis] = slice(None) if i < last else turn(me[axis], 4 - e) if i == last else me[axis]
        if part == 2:
            at["x"] = slice(None)
        return refs[part].at[at["x"], at["y"], at["z"], k]

    sent = []

    def push(ref, to, s_sem, r_sem):
        copy = pltpu.make_async_remote_copy(
            src_ref=ref, dst_ref=ref, send_sem=s_sem, recv_sem=r_sem, device_id=to, device_id_type=MESH
        )
        copy.start()
        sent.append(copy)
        return copy

    arrive = {}

    def phase(part, p, e):
        ref = view(part, p - 1, e) if p else view(part, 0, 0)
        for d in range(1, 4):
            arrive[part, p, e, d] = push(ref, peer(axes[part][p], d), send.at[part, p, e, d], recv.at[part, p, e, d])

    core = []

    def mate(part, e):
        core.append(push(view(part, 2, e), (r, at_col(y, z, 1 - k)), core_send.at[part, e], core_recv.at[part, e]))

    def corner(d):
        ref = lower.at[r - 2, y, z, k]
        return pltpu.make_async_remote_copy(
            src_ref=ref, dst_ref=ref, send_sem=send.at[2, 0, 0, d], recv_sem=recv.at[2, 0, 0, d], device_id=peer("x", d),
            device_id_type=MESH,
        )

    @pl.when(r >= 2)
    def _():
        for d in range(1, 4):
            corner(d).start()

    for part in range(2):
        phase(part, 0, 0)
    for part in range(2):
        phase(part, 1, 0)
    for e in range(1, 4):
        for part in range(2):
            arrive[part, 0, 0, e].wait_recv()
            phase(part, 1, e)
    for d in range(1, 4):
        @pl.when(turn(r, 4 - d) >= 2)
        def _(d=d):
            ref = lower.at[0, y, z, k]
            pltpu.make_async_remote_copy(
                src_ref=ref, dst_ref=ref, send_sem=send.at[2, 0, 0, d], recv_sem=recv.at[2, 0, 0, d], device_id=peer("x", d),
                device_id_type=MESH,
            ).wait_recv()
    phase(2, 1, 0)
    for part in (2, 0, 1):
        phase(part, 2, 0)
    for e in range(1, 4):
        for part in range(2):
            for f in range(4):
                arrive[part, 1, f, e].wait_recv()
            phase(part, 2, e)
        arrive[2, 1, 0, e].wait_recv()
        phase(2, 2, e)
    for part in range(3):
        mate(part, 0)
    for e in range(1, 4):
        for part in range(3):
            for f in range(4):
                arrive[part, 2, f, e].wait_recv()
            mate(part, e)

    def finish():
        for copy in core:
            copy.wait_recv()
        for copy in sent:
            copy.wait_send()

        @pl.when(r >= 2)
        def _():
            for d in range(1, 4):
                corner(d).wait_send()

    return finish


def main_body(slot_ref, mark_ref, mask_ref, front_ref, child_ref, out_ref, s, left, right, lower, own, labels, message, got, payload,
              tiles_ref, held, share, passed, g, across, arrived, high, low, m_send, m_recv, f_send, f_recv,
              a_send, a_recv, local_sem, x_send, x_recv, send, recv, core_send, core_recv,
              d_send, d_recv, dcore_send, dcore_recv):
    r, c, y, z, k = here()
    n_col = arrived.shape[0]
    lead = out_ref.shape[0]
    slab = TILE // n_col
    n = s.shape[1]
    fetch = pltpu.make_async_copy(front_ref.at[:, 0], held, local_sem.at[0])
    fetch.start()
    fill = pltpu.make_async_copy(child_ref, tiles_ref, local_sem.at[2])
    fill.start()
    peers = [(r, lax.rem(c + d, n_col)) for d in range(1, n_col)] + row_peers(r, c)
    barrier = pltpu.get_barrier_semaphore()
    for device in peers:
        pl.semaphore_signal(barrier, inc=1, device_id=device, device_id_type=MESH)
    sub = lax.broadcasted_iota(jnp.int32, (slab, 128), 0)
    base = jnp.zeros((slab, 128), jnp.float32)
    for q in range(4):
        base = jnp.where(sub == q, mark_ref[q], base)
    for q in range(n_col):
        message[q, :, 5 * TILE:] = jnp.where(sub == 4, mark_ref[q], base)
    fetch.wait()
    message[:, :, 4 * TILE:5 * TILE] = held[:TILE].T.reshape(n_col, slab, TILE)
    fill.wait()
    for q in range(4):
        message[:, :, q * TILE:(q + 1) * TILE] = tiles_ref[slot_ref[q]].reshape(n_col, slab, TILE)
    got[c] = message[c]
    pl.semaphore_wait(barrier, len(peers))

    def letter(d):
        dy, dz, dk = MOVES[d]
        to = at_col(turn(y, dy), turn(z, dz), lax.rem(k + dk, 2))
        return pltpu.make_async_remote_copy(
            src_ref=message.at[to], dst_ref=got.at[c], send_sem=m_send.at[d], recv_sem=m_recv.at[d], device_id=(r, to),
            device_id_type=MESH,
        )

    letters = [letter(d) for d in range(1, n_col)]
    for copy in letters:
        copy.start()
    for q in range(n_col):
        payload[q] = tiles_ref[slot_ref[q]]

    def tile(d):
        dy, dz, dk = MOVES[d]
        to = at_col(turn(y, dy), turn(z, dz), lax.rem(k + dk, 2))
        return to, pltpu.make_async_remote_copy(
            src_ref=payload.at[to],
            dst_ref=arrived.at[d],
            send_sem=a_send.at[d],
            recv_sem=a_recv.at[d],
            device_id=(r, to),
            device_id_type=MESH,
        )

    def begin(ds):
        for d in range(*ds):
            to, copy = tile(d)

            @pl.when(to >= 4)
            def _(copy=copy):
                copy.start()

    begin(STARTS[-2])
    arrived[0] = payload[c]
    for t in range(lead):
        out_ref[t] = held[t * TILE:(t + 1) * TILE]
    for copy in letters:
        copy.wait_recv()

    def exchange(src, dst, s_sem, r_sem, d):
        return pltpu.make_async_remote_copy(
            src_ref=src, dst_ref=dst, send_sem=s_sem.at[d], recv_sem=r_sem.at[d], device_id=(turn(r, d), c),
            device_id_type=MESH,
        )

    for q in range(4):
        for t in range(lead):
            share[q, t] = got[4 * t + q, :, 4 * TILE:5 * TILE]
    passed[r] = share[r]
    shares = [exchange(share.at[turn(r, d)], passed.at[r], f_send, f_recv, d) for d in range(1, 4)]
    for copy in shares:
        copy.start()
    labels[...] = got[:, 4, 5 * TILE:5 * TILE + 128]
    own[...] = jnp.zeros_like(own)

    def add(i, carry):
        for q in range(4):
            at = slice(q * TILE, (q + 1) * TILE)
            acc = [own[t * slab:(t + 1) * slab, at] for t in range(lead)]
            for e in range(8):
                label = got[i * 8 + e, q:q + 1, 5 * TILE:5 * TILE + 128]
                label = jnp.broadcast_to(jnp.concatenate([label, label], axis=1), (slab, TILE))
                part_in = got[i * 8 + e, :, at]
                for t in range(lead):
                    acc[t] = acc[t] + jnp.where(label == float(t), part_in, 0.0)
            for t in range(lead):
                own[t * slab:(t + 1) * slab, at] = acc[t]
        return carry

    lax.fori_loop(0, n_col // 8, add, 0)
    for copy in shares:
        copy.wait_recv()
    for q in range(4):
        at = slice(q * TILE, (q + 1) * TILE)
        for t in range(lead):
            rows = slice(t * slab, (t + 1) * slab)
            own[rows, at] = own[rows, at] + passed[q, t]
    left[r, y, z, k] = own[:slab, :TILE]
    right[r, y, z, k] = own[:slab, TILE:2 * TILE]

    @pl.when(r >= 2)
    def _():
        lower[r - 2, y, z, k] = own[:slab, 2 * TILE:]

    close = cube_gather(left, right, lower, d_send, d_recv, dcore_send, dcore_recv, r, y, z, k)
    begin(STARTS[-1])
    close()
    row0 = load_diag(left, right, lower, own, mask_ref, s)
    for step in range(n // NB):
        factor_step(s, step)
        if step in STARTS:
            begin(STARTS[step])
    m = s.shape[0] - n
    ids = lax.broadcasted_iota(jnp.int32, (m, n), 0)
    lane = lax.broadcasted_iota(jnp.int32, (m, n), 1)
    mine = jnp.where((ids >= 8) | (lane <= ids + row0), s[n:, :], 0.0)
    g[y, z, k] = mine.reshape(g.shape[3:])

    half = lead // 2

    def piece(h, yy, zz, kk):
        return g.at[yy, zz, kk, pl.ds(h * half, half)]

    t_of = lax.div(c, 4)
    source = lax.rem(c, 4)
    part = lax.div(t_of, half)

    def cross(h, da, mate, d):
        kk = lax.rem(k + mate, 2)
        if h == 0:
            zz = turn(z, 4 - da)
            src, dst = g.at[:, zz, kk, t_of], across.at[:, zz, kk]
        else:
            yy = turn(y, 4 - da)
            src, dst = g.at[yy, :, kk, t_of], across.at[yy, :, kk]
        return pltpu.make_async_remote_copy(
            src_ref=src, dst_ref=dst, send_sem=x_send.at[mate, da, d], recv_sem=x_recv.at[mate, da],
            device_id=(turn(r, d), c), device_id_type=MESH,
        )

    def forward(da, mate):
        for h in range(2):
            @pl.when((r == source) & (part == h))
            def _(h=h):
                for d in range(1, 4):
                    cross(h, da, mate, d).start()

    def early():
        begin(EARLY)

    finish = plane_gather(piece, send, recv, core_send, core_recv, r, y, z, k, early, forward)
    begin(LATER)

    def absorb(ds):
        @pl.when(c >= 4)
        def _():
            for d in ds:
                if d:
                    tile(d)[1].wait_recv()
            wanted = []
            for d in ds:
                dy, dz, dk = MOVES[d]
                origin = at_col(turn(y, 4 - dy), turn(z, 4 - dz), lax.rem(k + dk, 2))
                wanted.append(jnp.concatenate([labels[pl.ds(origin, 1), :]] * 2, axis=1))

            def strip(i, carry):
                rows = pl.ds(pl.multiple_of(i * 8, 8), 8)
                acc = [out_ref[t, rows, :] for t in range(lead)]
                for d, want in zip(ds, wanted):
                    part_in = arrived[d, rows, :]
                    want = jnp.broadcast_to(want, (8, TILE))
                    for t in range(lead):
                        acc[t] = acc[t] + jnp.where(want == float(t), part_in, 0.0)
                for t in range(lead):
                    out_ref[t, rows, :] = acc[t]
                return carry

            lax.fori_loop(0, TILE // 8, strip, 0)

    absorb(range(0, 10))
    absorb(range(10, 18))
    finish()

    @pl.when(r == source)
    def _():
        local_copy = pltpu.make_async_copy(g.at[:, :, :, t_of], across, local_sem.at[1])
        local_copy.start()
        local_copy.wait()

    for h in range(2):
        @pl.when((r != source) & (part == h))
        def _(h=h):
            for mate in range(2):
                for da in range(4):
                    cross(h, da, mate, 1).wait_recv()

    @pl.when(c < 4)
    def _():
        at = pl.multiple_of(jnp.minimum(c, 3) * TILE, TILE)
        for t in range(lead):
            out_ref[t] = g[:, :, :, t, :, pl.ds(at, TILE)].reshape(TILE, TILE)

    @pl.when(c >= 4)
    def _():
        high[...], low[...] = split(across[...].reshape(TILE, n))

        def update(t, carry):
            ah, al = split(g[:, :, :, t].reshape(TILE, n))
            out_ref[t] = out_ref[t] - (nt(ah, high[...]) + (nt(ah, low[...]) + nt(al, high[...])))
            return carry

        lax.fori_loop(1, lead, update, 0)

    for lo, hi in ((18, 24), (24, 28), (28, 32)):
        absorb(range(lo, hi))

    @pl.when(c >= 4)
    def _():
        out_ref[0] = jnp.zeros((TILE, TILE), jnp.float32)

    for d in range(1, n_col):
        to, copy = tile(d)

        @pl.when(to >= 4)
        def _(copy=copy):
            copy.wait_send()

    for h in range(2):
        @pl.when((r == source) & (part == h))
        def _(h=h):
            for mate in range(2):
                for da in range(4):
                    for d in range(1, 4):
                        cross(h, da, mate, d).wait_send()
    for copy in letters + shares:
        copy.wait_send()


def main_call(slots, marks, mask, front, tiles):
    n_col = tiles.shape[0]
    slab = TILE // n_col
    n = 4 * TILE
    lead = front.shape[0] // TILE
    dma = pltpu.SemaphoreType.DMA
    f32 = jnp.float32
    smem = pl.BlockSpec(memory_space=pltpu.SMEM)
    return pl.pallas_call(
        main_body,
        out_shape=jax.ShapeDtypeStruct((lead, TILE, TILE), f32),
        in_specs=[smem] * 3 + [pl.BlockSpec(memory_space=pl.ANY)] * 2,
        out_specs=pl.BlockSpec(memory_space=pltpu.VMEM),
        scratch_shapes=[
            pltpu.VMEM((n + lead * slab, n), f32),
            pltpu.VMEM((4, 4, 4, 2, slab, TILE), f32),
            pltpu.VMEM((4, 4, 4, 2, slab, TILE), f32),
            pltpu.VMEM((2, 4, 4, 2, slab, 2 * TILE), f32),
            pltpu.VMEM((lead * slab, n), f32),
            pltpu.VMEM((n_col, 128), f32),
            pltpu.VMEM((n_col, slab, 5 * TILE + 128), f32),
            pltpu.VMEM((n_col, slab, 5 * TILE + 128), f32),
            pltpu.VMEM(tiles.shape, f32),
            pltpu.VMEM(tiles.shape, f32),
            pltpu.VMEM((lead * TILE, TILE), f32),
            pltpu.VMEM((4, lead, slab, TILE), f32),
            pltpu.VMEM((4, lead, slab, TILE), f32),
            pltpu.VMEM((4, 4, 2, lead, slab, n), f32),
            pltpu.VMEM((4, 4, 2, slab, n), f32),
            pltpu.VMEM((n_col, TILE, TILE), f32),
            pltpu.VMEM((TILE, n), jnp.bfloat16),
            pltpu.VMEM((TILE, n), jnp.bfloat16),
            dma((n_col,)),
            dma((n_col,)),
            dma((4,)),
            dma((4,)),
            dma((n_col,)),
            dma((n_col,)),
            dma((3,)),
            dma((2, 4, 4)),
            dma((2, 4)),
        ]
        + gather_sems()
        + [dma((3, 3, 4, 4)), dma((3, 3, 4, 4)), dma((3, 4)), dma((3, 4))],
        compiler_params=pltpu.CompilerParams(collective_id=0, has_side_effects=True, vmem_limit_bytes=60 * MIB),
        cost_estimate=pl.CostEstimate(flops=0, bytes_accessed=1000, transcendentals=0),
    )(slots, marks, mask, front, tiles)


def store_body(in_ref, out_ref, sem):
    copies = [
        pltpu.make_async_copy(in_ref.at[t], out_ref.at[pl.ds(t * TILE, TILE), 0], sem.at[t]) for t in range(in_ref.shape[0])
    ]
    for copy in copies:
        copy.start()
    for copy in copies:
        copy.wait()


def store_call(x):
    lead = x.shape[0]
    return pl.pallas_call(
        store_body,
        out_shape=jax.ShapeDtypeStruct((lead * TILE, 1, TILE), x.dtype),
        in_specs=[pl.BlockSpec(memory_space=pltpu.VMEM)],
        out_specs=pl.BlockSpec(memory_space=pl.ANY),
        scratch_shapes=[pltpu.SemaphoreType.DMA((lead,))],
    )(x)


def local(front, child_tiles, child_owner, child_place, child_count, tile_mask):
    n_col = lax.axis_size("col")
    lead = front.shape[0]
    slots = child_tiles.shape[2]
    owner = child_owner.reshape(slots)
    place = child_place.reshape(slots)
    count = child_count.reshape(())
    ids = jnp.arange(slots, dtype=jnp.int32)
    hit = owner[None, :] == jnp.arange(n_col, dtype=jnp.int32)[:, None]
    slot_of = jnp.sum(jnp.where(hit, ids[None, :], 0), axis=1)
    marks = (jnp.sum(jnp.where(hit & (ids < count)[None, :], place[None, :] + 1, 0), axis=1) - 1).astype(jnp.float32)
    result = main_call(slot_of, marks, tile_mask, front.reshape(lead * TILE, 1, TILE), child_tiles.reshape(slots, TILE, TILE))
    return store_call(result).reshape(front.shape)


def solution(mesh):
    return jax.shard_map(
        local,
        mesh=mesh,
        in_specs=(
            P(None, "row", None, None, "col", None),
            P("row", "col", None, None, None),
            P("row", "col", None),
            P("row", "col", None),
            P("row", "col"),
            P(),
        ),
        out_specs=P(None, "row", None, None, "col", None),
        check_vma=False,
    )
```
